1024 devices in a mesh: row: 64 (over z, core), col: 16 (over x, y).
Axes of the slice: x: 4, y: 4, z: 32, core: 2. Of those that a mesh axis runs over, the one named last changes fastest.
Arguments:
- eigvecs: float32 [49152, 2048], P(('row', 'col')), may hold values from -6 to 6
- reflectors: float32 [3, 49152, 512], P(None, 'row'), may hold values from -0.15625 to 0.15625
- t_factor: float32 [3, 512, 512], replicated, as said below
- offsets: int32 [3], replicated, may hold values from 0 to 48640, as said below
Outputs:
- updated: float32 [49152, 2048], P('row', 'col')
The draws below stay inside these ranges and needn't reach their ends.
Inputs may be any that keep to these rules, and one draw needn't show every extreme that they name: Each panel's vectors begin on consecutive rows offsets[p] to offsets[p] + 511; some panel starts at row 0 and some at row 48640. `t_factor`: each panel's factor is upper triangular with a diagonal between 0.25 and 2.
All inputs are finite; a program needn't handle non-finite values.
Results may differ from the reference program's by a relative error of at most 0.00014.
Values sent between devices are 32-bit elements; how exact they have to be, the bound alone decides.
A program may use at most 32 MiB of HBM per device.

```python
import jax
import jax.numpy as jnp
from jax import lax

K = 2048
PANEL = 512
PANELS = 3
N = 49152


def draw_t_factor(key, part):
    key_diag = jax.random.fold_in(key, 11)
    key_off = jax.random.fold_in(key, 12)
    diagonal = jax.random.uniform(key_diag, (PANELS, PANEL), jnp.float32, 0.5, 1.5)
    upper = jax.random.normal(key_off, (PANELS, PANEL, PANEL), jnp.float32) * (0.6 / PANEL ** 0.5)
    rows = lax.broadcasted_iota(jnp.int32, (1, PANEL, PANEL), 1)
    cols = lax.broadcasted_iota(jnp.int32, (1, PANEL, PANEL), 2)
    strict = jnp.where(cols > rows, upper, jnp.float32(0.0))
    return strict + jnp.where(cols == rows, diagonal[:, :, None], jnp.float32(0.0))


def draw_offsets(key, part):
    starts = jax.random.randint(jax.random.fold_in(key, 21), (PANELS,), 0, N - PANEL + 1, jnp.int32)
    order = jax.random.permutation(jax.random.fold_in(key, 22), PANELS).astype(jnp.int32)
    which = lax.broadcasted_iota(jnp.int32, (PANELS,), 0)
    starts = jnp.where(which == order[0], jnp.int32(N - PANEL), starts)
    starts = jnp.where(which == order[1], jnp.int32(0), starts)
    return starts.astype(jnp.int32)


def level_of(key, shape, cuts, least, largest):
    level = 1.0
    for dim, blocks in cuts:
        steps = jax.random.uniform(jax.random.fold_in(jax.random.fold_in(key, 6), dim), (blocks,), jnp.float32, least / len(cuts), largest / len(cuts))
        level = level * jnp.repeat(jnp.exp(steps), shape[dim] // blocks).reshape((-1,) + (1,) * (len(shape) - 1 - dim))
    return level


def noise(rng, shape, deviation, bound, pieces=(), held_as=jnp.bfloat16):
    values = deviation * jax.random.normal(rng, shape, jnp.float32)
    if pieces:
        values = values * level_of(rng, shape, pieces, -0.22, 0.18)
    return jnp.clip(values, -bound, bound).astype(held_as)


def setup_inputs(seed: int = 0) -> dict:
    keys = jax.random.split(jax.random.key(seed), 5)
    eigvecs = noise(keys[0], (N, K), 1.0, 6.0, ((0, 1024),), jnp.float32)
    reflectors = noise(keys[1], (PANELS, N, PANEL), (N // 32) ** -0.5, 0.15625, ((1, 64),), jnp.float32)
    t_factor = draw_t_factor(jax.random.fold_in(keys[4], 71), 0)
    offsets = draw_offsets(jax.random.fold_in(keys[4], 71), 0)
    return dict(eigvecs=eigvecs, reflectors=reflectors, t_factor=t_factor, offsets=offsets)


def reference(eigvecs, reflectors, t_factor, offsets):
    row_index = lax.broadcasted_iota(jnp.int32, (N, 1), 0)
    column = lax.broadcasted_iota(jnp.int32, (1, PANEL), 1)
    current = eigvecs
    for panel in range(PANELS):
        starts = (offsets[panel].astype(jnp.int32) + column).astype(jnp.int32)
        vectors = jnp.where(row_index > starts, reflectors[panel],
                            jnp.where(row_index == starts, jnp.float32(1.0), jnp.float32(0.0)))
        inner = lax.dot_general(vectors, current, (((0,), (0,)), ((), ())),
                                precision=lax.Precision.HIGHEST, preferred_element_type=jnp.float32)
        scaled = jnp.dot(t_factor[panel], inner, precision=lax.Precision.HIGHEST,
                         preferred_element_type=jnp.float32)
        current = current - jnp.dot(vectors, scaled, precision=lax.Precision.HIGHEST,
                                    preferred_element_type=jnp.float32)
    return current
```

```python
import jax
import jax.numpy as jnp
from jax import lax
from jax.experimental import pallas as pl
from jax.experimental.pallas import tpu as pltpu
from jax.sharding import PartitionSpec as P

MESH = pl.DeviceIdType.MESH
F32 = jnp.float32
BF16 = jnp.bfloat16

NX, NY, NZ = 4, 4, 32
ROWS, PANEL, COLS = 768, 512, 128
PIECE = 48
TAIL = ROWS - PANEL
LAST = 64 * ROWS - PANEL
NEAR = (4, 3, -3, 2, -2, 1, -1)
FAR = (16, 8, -8)
XY = tuple((a, b) for a in range(NX) for b in range(NY) if (a, b) != (0, 0))
CHUNK = COLS // 8
GCHUNK = 8


def split(value):
    hi = value.astype(BF16)
    return hi, (value - hi.astype(F32)).astype(BF16)


def mm(a, b):
    return lax.dot_general(a, b, (((1,), (0,)), ((), ())), preferred_element_type=F32)


def mm_nt(a, b):
    return lax.dot_general(a, b, (((1,), (1,)), ((), ())), preferred_element_type=F32)


def mm_tn(a, b):
    return lax.dot_general(a, b, (((0,), (0,)), ((), ())), preferred_element_type=F32)


def three(dot, ah, al, bh, bl):
    return dot(ah, bh) + (dot(ah, bl) + dot(al, bh))


def kernel(
    off_ref, x_hbm, v_hbm, t_hbm, out_ref,
    cur, v3, t3, vh, vl, ch, cl, th, tl, ph, pl_, xs, w2, wpair, wsum, wrs, wx, wmine, wfull,
    gpart, gpair, gsum, grs, gx, gmine, gfull,
    load_sem, own_sem, a2a_s, a2a_r, gp_s, gp_r, wp_s, wp_r, grs_s, grs_r, wrs_s, wrs_r,
    gx_s, gx_r, wx_s, wx_r, gag_s, gag_r, wag_s, wag_r, gxy_s, gxy_r, gc_s, gc_r, wc_s, wc_r, far_sem,
):
    row, col = lax.axis_index("row"), lax.axis_index("col")
    z, core = row // 2, lax.rem(row, 2)
    x, y = col // NY, lax.rem(col, NY)
    other = 1 - core

    def along_z(d):
        return (lax.rem(z + (d + NZ), NZ) * 2 + core, col)

    def in_plane(a, b):
        return (row, lax.rem(x + a, NX) * NY + lax.rem(y + b, NY))

    partner = (z * 2 + other, col)

    def remote(src, dst, ssem, rsem, to):
        copy = pltpu.make_async_remote_copy(
            src_ref=src, dst_ref=dst, send_sem=ssem, recv_sem=rsem, device_id=to, device_id_type=MESH
        )
        copy.start()
        return copy

    barrier = pltpu.get_barrier_semaphore()
    greet = [in_plane(a, b) for a, b in XY] + [along_z(d) for d in (4, -4, 3, -3, 2, -2, 1, -1)] + [partner]
    for to in greet:
        pl.semaphore_signal(barrier, inc=1, device_id=to, device_id_type=MESH)

    loads = [pltpu.make_async_copy(v_hbm.at[p], v3.at[p], load_sem.at[p]) for p in range(3)]
    loads += [pltpu.make_async_copy(t_hbm, t3, load_sem.at[3])]
    for load in loads:
        load.start()
    mine = pl.ds(pl.multiple_of(col * PIECE, PIECE), PIECE)
    own = pltpu.make_async_copy(
        x_hbm.at[:, pl.ds(pl.multiple_of(col * COLS, COLS), COLS)], cur.at[mine, :], own_sem
    )
    own.start()

    pl.semaphore_wait(barrier, len(greet))
    a2a = []
    for n, (a, b) in enumerate(XY):
        to = in_plane(a, b)
        src = x_hbm.at[:, pl.ds(pl.multiple_of(to[1] * COLS, COLS), COLS)]
        a2a.append(remote(src, cur.at[mine, :], a2a_s.at[n], a2a_r.at[n], to))
    for d in (4, -4):
        pl.semaphore_signal(far_sem.at[0], inc=1, device_id=along_z(d), device_id_type=MESH)

    c = jnp.where(off_ref[0] == LAST, 0, jnp.where(off_ref[1] == LAST, 1, 2))
    pa = jnp.where(c == 0, 1, 0)
    pb = jnp.where(c == 2, 1, 2)
    off_a, off_b = off_ref[pa], off_ref[pb]

    def masked(panel, start, first, count):
        value = v3[panel, pl.ds(first, count), :]
        step = (
            row * ROWS + first - start
            + lax.broadcasted_iota(jnp.int32, (count, PANEL), 0)
            - lax.broadcasted_iota(jnp.int32, (count, PANEL), 1)
        )
        return jnp.where(step > 0, value, jnp.where(step == 0, F32(1.0), F32(0.0)))

    for load in loads:
        load.wait()

    R = 64

    def prepare(i, _):
        first = pl.multiple_of(i * R, R)
        hi, lo = split(masked(pa, off_a, first, R))
        vh[0, pl.ds(first, R), :] = hi
        vl[0, pl.ds(first, R), :] = lo
        hi, lo = split(masked(pb, off_b, first, R))
        vh[1, pl.ds(first, R), :] = hi
        vl[1, pl.ds(first, R), :] = lo
        vh[2, pl.ds(first, R), :] = hi
        vl[2, pl.ds(first, R), :] = lo
        return 0

    lax.fori_loop(0, ROWS // R, prepare, 0)

    def prepare_c(i, _):
        first = pl.multiple_of(i * R, R)
        hi, lo = split(masked(c, LAST, TAIL + first, R))
        ch[pl.ds(first, R), :] = hi
        cl[pl.ds(first, R), :] = lo
        for s, panel in ((0, pa), (1, pb), (2, c)):
            hi, lo = split(t3[panel, pl.ds(first, R), :])
            th[s, pl.ds(first, R), :] = hi
            tl[s, pl.ds(first, R), :] = lo
        return 0

    lax.fori_loop(0, PANEL // R, prepare_c, 0)

    M = 128

    def project(i, _):
        rows = pl.ds(pl.multiple_of(i * M, M), M)
        hi, lo = split(three(mm, ch[rows, :], cl[rows, :], th[2], tl[2]))
        hi, lo = split(three(mm_nt, hi, lo, ch[...], cl[...]))
        ph[rows, :] = hi
        pl_[rows, :] = lo
        return 0

    lax.fori_loop(0, PANEL // M, project, 0)

    def through(i, _):
        cols = pl.ds(pl.multiple_of(i * M, M), M)
        rows = pl.ds(pl.multiple_of(TAIL + i * M, M), M)
        tail = pl.ds(TAIL, PANEL)
        moved = three(mm_tn, ph[:, cols], pl_[:, cols], vh[2, tail, :], vl[2, tail, :])
        value = masked(pb, off_b, TAIL + i * M, M)
        hi, lo = split(jnp.where(c == 1, value - moved, value))
        vh[1, rows, :] = hi
        vl[1, rows, :] = lo
        return 0

    lax.fori_loop(0, PANEL // M, through, 0)

    gi, gj = x, y
    bi = pl.ds(pl.multiple_of(gi * 128, 128), 128)
    bj = pl.ds(pl.multiple_of(gj * 128, 128), 128)
    gpart[...] = three(mm_tn, vh[1, :, bi], vl[1, :, bi], vh[0, :, bj], vl[0, :, bj])
    gp = remote(gpart.at[pl.ds(pl.multiple_of(other * 64, 64), 64), :], gpair, gp_s, gp_r, partner)

    pl.semaphore_wait(far_sem.at[0], 2)
    for d in (8, -8):
        pl.semaphore_signal(far_sem.at[1], inc=1, device_id=along_z(d), device_id_type=MESH)

    gp.wait()
    gsum[...] = gpart[pl.ds(pl.multiple_of(core * 64, 64), 64), :] + gpair[...]
    slot = lax.rem(z, 8)

    def slot_of(d):
        return lax.rem(z + (d + NZ), 8)

    g_rs = []
    for n, d in enumerate(NEAR):
        src = gsum.at[pl.ds(pl.multiple_of(slot_of(d) * GCHUNK, GCHUNK), GCHUNK), :]
        g_rs.append(remote(src, grs.at[n], grs_s.at[n], grs_r.at[n], along_z(d)))

    own.wait()
    for copy in a2a:
        copy.wait()
    tail = pl.ds(TAIL, PANEL)
    xh, xl = split(cur[tail, :])
    moved = three(mm, ph[...], pl_[...], xh, xl)
    cur[tail, :] = jnp.where(c == 0, cur[tail, :] - moved, cur[tail, :])
    hi, lo = split(cur[...].T)
    xs[pl.ds(0, COLS), :] = hi
    xs[pl.ds(COLS, COLS), :] = lo

    def inner(p):
        both = mm(xs[...], vh[p])
        w2[p] = both[:COLS] + both[COLS:] + mm(xs[pl.ds(0, COLS), :], vl[p])

    inner(other)
    wp = remote(w2.at[other], wpair, wp_s, wp_r, partner)
    inner(core)
    wp.wait()
    wsum[...] = w2[core] + wpair[...]
    w_rs = []
    for n, d in enumerate(NEAR):
        src = wsum.at[pl.ds(pl.multiple_of(slot_of(d) * CHUNK, CHUNK), CHUNK), :]
        w_rs.append(remote(src, wrs.at[n], wrs_s.at[n], wrs_r.at[n], along_z(d)))

    for copy in g_rs:
        copy.wait()
    total = gsum[pl.ds(pl.multiple_of(slot * GCHUNK, GCHUNK), GCHUNK), :]
    for n in range(len(NEAR)):
        total = total + grs[n]
    gmine[...] = total
    pl.semaphore_wait(far_sem.at[1], 2)
    g_x = [remote(gmine, gx.at[n], gx_s.at[n], gx_r.at[n], along_z(d)) for n, d in enumerate(FAR)]

    for copy in w_rs:
        copy.wait()
    total = wsum[pl.ds(pl.multiple_of(slot * CHUNK, CHUNK), CHUNK), :]
    for n in range(len(NEAR)):
        total = total + wrs[n]
    wmine[...] = total
    w_x = [remote(wmine, wx.at[n], wx_s.at[n], wx_r.at[n], along_z(d)) for n, d in enumerate(FAR)]

    for copy in g_x:
        copy.wait()
    ghalf = gi * 128 + core * 64
    gspot = (pl.ds(pl.multiple_of(ghalf + slot * GCHUNK, GCHUNK), GCHUNK), bj)
    gfull[gspot] = (gmine[...] + gx[0]) + (gx[1] + gx[2])
    g_ag = [
        remote(gfull.at[gspot], gfull.at[gspot], gag_s.at[n], gag_r.at[n], along_z(d))
        for n, d in enumerate(NEAR)
    ]
    for copy in g_ag:
        copy.wait()
    gown = gfull.at[pl.ds(pl.multiple_of(ghalf, 64), 64), bj]
    g_xy = [remote(gown, gown, gxy_s.at[n], gxy_r.at[n], in_plane(a, b)) for n, (a, b) in enumerate(XY)]

    for copy in w_x:
        copy.wait()
    wspot = pl.ds(pl.multiple_of(slot * CHUNK, CHUNK), CHUNK)
    wfull[core, wspot, :] = (wmine[...] + wx[0]) + (wx[1] + wx[2])
    w_ag = [
        remote(wfull.at[core, wspot, :], wfull.at[core, wspot, :], wag_s.at[n], wag_r.at[n], along_z(d))
        for n, d in enumerate(NEAR)
    ]
    for copy in g_xy:
        copy.wait()
    g_c = []
    for i in range(4):
        part = gfull.at[pl.ds(pl.multiple_of(i * 128 + core * 64, 64), 64), :]
        g_c.append(remote(part, part, gc_s.at[i], gc_r.at[i], partner))
    for copy in w_ag:
        copy.wait()
    w_c = remote(wfull.at[core], wfull.at[core], wc_s, wc_r, partner)
    for copy in g_c:
        copy.wait()
    w_c.wait()

    hi, lo = split(wfull[0])
    sa = three(mm_nt, hi, lo, th[0], tl[0])
    sah, sal = split(sa)
    gh, gl = split(gfull[...])
    rest = wfull[1] - three(mm_nt, sah, sal, gh, gl)
    hi, lo = split(rest)
    sb = three(mm_nt, hi, lo, th[1], tl[1])
    sbh, sbl = split(sb)

    def update(p, value, sh, sl):
        both = mm_nt(vh[p], jnp.concatenate([sh, sl], axis=0))
        return value - (both[:, :COLS] + both[:, COLS:] + mm_nt(vl[p], sh))

    after_a = update(0, cur[...], sah, sal)
    cur[...] = after_a
    out_ref[...] = update(2, after_a, sbh, sbl)
    through_c = jnp.where(c == 1, cur[tail, :], out_ref[tail, :])
    xh, xl = split(through_c)
    moved = three(mm, ph[...], pl_[...], xh, xl)
    out_ref[tail, :] = jnp.where(c == 0, out_ref[tail, :], out_ref[tail, :] - moved)


def per_device(eigvecs, reflectors, t_factor, offsets):
    dma = pltpu.SemaphoreType.DMA
    near, far, plane = len(NEAR), len(FAR), len(XY)
    hbm, vmem = pl.BlockSpec(memory_space=pl.ANY), pltpu.VMEM
    return pl.pallas_call(
        kernel,
        out_shape=jax.ShapeDtypeStruct((ROWS, COLS), F32),
        in_specs=[pl.BlockSpec(memory_space=pltpu.SMEM), hbm, hbm, hbm],
        out_specs=pl.BlockSpec(memory_space=pltpu.VMEM),
        scratch_shapes=[
            vmem((ROWS, COLS), F32),
            vmem((3, ROWS, PANEL), F32),
            vmem((3, PANEL, PANEL), F32),
            vmem((3, ROWS, PANEL), BF16),
            vmem((3, ROWS, PANEL), BF16),
            vmem((PANEL, PANEL), BF16),
            vmem((PANEL, PANEL), BF16),
            vmem((3, PANEL, PANEL), BF16),
            vmem((3, PANEL, PANEL), BF16),
            vmem((PANEL, PANEL), BF16),
            vmem((PANEL, PANEL), BF16),
            vmem((2 * COLS, ROWS), BF16),
            vmem((2, COLS, PANEL), F32),
            vmem((COLS, PANEL), F32),
            vmem((COLS, PANEL), F32),
            vmem((near, CHUNK, PANEL), F32),
            vmem((far, CHUNK, PANEL), F32),
            vmem((CHUNK, PANEL), F32),
            vmem((2, COLS, PANEL), F32),
            vmem((128, 128), F32),
            vmem((64, 128), F32),
            vmem((64, 128), F32),
            vmem((near, GCHUNK, 128), F32),
            vmem((far, GCHUNK, 128), F32),
            vmem((GCHUNK, 128), F32),
            vmem((PANEL, PANEL), F32),
            dma((4,)), dma, dma((plane,)), dma((plane,)), dma, dma, dma, dma,
            dma((near,)), dma((near,)), dma((near,)), dma((near,)),
            dma((far,)), dma((far,)), dma((far,)), dma((far,)),
            dma((near,)), dma((near,)), dma((near,)), dma((near,)),
            dma((plane,)), dma((plane,)), dma((4,)), dma((4,)), dma, dma,
            pltpu.SemaphoreType.REGULAR((2,)),
        ],
        compiler_params=pltpu.CompilerParams(
            collective_id=0, has_side_effects=True, vmem_limit_bytes=48 * 2**20
        ),
        cost_estimate=pl.CostEstimate(flops=3 * 10**9, bytes_accessed=9 * 10**6, transcendentals=0),
        name="panels",
    )(offsets, eigvecs, reflectors, t_factor)


def solution(mesh):
    return jax.shard_map(
        per_device,
        mesh=mesh,
        in_specs=(P(("row", "col"), None), P(None, "row", None), P(), P()),
        out_specs=P("row", "col"),
        check_vma=False,
    )
```

```python
import jax
import jax.numpy as jnp
from jax import lax
from jax.experimental import pallas as pl
from jax.experimental.pallas import tpu as pltpu
from jax.sharding import PartitionSpec as P

MESH = pl.DeviceIdType.MESH
F32 = jnp.float32
BF16 = jnp.bfloat16

NX, NY, NZ = 4, 4, 32
ROWS, PANEL, COLS = 768, 512, 128
PIECE = 48
TAIL = ROWS - PANEL
LAST = 64 * ROWS - PANEL
NEAR = (4, 3, -3, 2, -2, 1, -1)
FAR = (16, 8, -8)
XY = tuple((a, b) for a in range(NX) for b in range(NY) if (a, b) != (0, 0))
HALF = COLS // 2
CHUNK = HALF // 8
GCHUNK = 8


def split(value):
    hi = value.astype(BF16)
    return hi, (value - hi.astype(F32)).astype(BF16)


def mm(a, b):
    return lax.dot_general(a, b, (((1,), (0,)), ((), ())), preferred_element_type=F32)


def mm_nt(a, b):
    return lax.dot_general(a, b, (((1,), (1,)), ((), ())), preferred_element_type=F32)


def mm_tn(a, b):
    return lax.dot_general(a, b, (((0,), (0,)), ((), ())), preferred_element_type=F32)


def three(dot, ah, al, bh, bl):
    return dot(ah, bh) + (dot(ah, bl) + dot(al, bh))


def kernel(
    off_ref, x_hbm, v_hbm, t_hbm, out_ref,
    xv, cur, v3, t3, vh, vl, qh, ql, ch, cl, th, tl, ph, pl_, xs, w2, wpair, wsum, wrs, wx, wmine, wfull,
    gpart, gpair, gsum, grs, gx, gmine, gfull,
    load_sem, own_sem, a2a_s, a2a_r, gp_s, gp_r, wp_s, wp_r, grs_s, grs_r, wrs_s, wrs_r,
    gx_s, gx_r, wx_s, wx_r, gag_s, gag_r, wag_s, wag_r, gxy_s, gxy_r, gc_s, gc_r, wc_s, wc_r, far0, far1,
):
    row, col = lax.axis_index("row"), lax.axis_index("col")
    z, core = row // 2, lax.rem(row, 2)
    x, y = col // NY, lax.rem(col, NY)
    other = 1 - core

    def along_z(d):
        return (lax.rem(z + (d + NZ), NZ) * 2 + core, col)

    def in_plane(a, b):
        return (row, lax.rem(x + a, NX) * NY + lax.rem(y + b, NY))

    partner = (z * 2 + other, col)

    def remote(src, dst, ssem, rsem, to):
        copy = pltpu.make_async_remote_copy(
            src_ref=src, dst_ref=dst, send_sem=ssem, recv_sem=rsem, device_id=to, device_id_type=MESH
        )
        copy.start()
        return copy

    barrier = pltpu.get_barrier_semaphore()
    greet = [in_plane(a, b) for a, b in XY] + [along_z(d) for d in (4, -4, 3, -3, 2, -2, 1, -1)] + [partner]
    for to in greet:
        pl.semaphore_signal(barrier, inc=1, device_id=to, device_id_type=MESH)

    xload = pltpu.make_async_copy(x_hbm, xv, load_sem.at[0])
    xload.start()
    vloads = [pltpu.make_async_copy(v_hbm.at[p], v3.at[p], load_sem.at[1 + p]) for p in range(3)]
    tload = pltpu.make_async_copy(t_hbm, t3, load_sem.at[4])
    for load in vloads + [tload]:
        load.start()

    c = jnp.where(off_ref[0] == LAST, 0, jnp.where(off_ref[1] == LAST, 1, 2))
    pa = jnp.where(c == 0, 1, 0)
    pb = jnp.where(c == 2, 1, 2)
    off_a, off_b = off_ref[pa], off_ref[pb]

    def masked(panel, start, first, count):
        value = v3[panel, pl.ds(first, count), :]
        step = (
            row * ROWS + first - start
            + lax.broadcasted_iota(jnp.int32, (count, PANEL), 0)
            - lax.broadcasted_iota(jnp.int32, (count, PANEL), 1)
        )
        return jnp.where(step > 0, value, jnp.where(step == 0, F32(1.0), F32(0.0)))

    mine = pl.ds(pl.multiple_of(col * PIECE, PIECE), PIECE)
    xload.wait()
    own = pltpu.make_async_copy(
        xv.at[:, pl.ds(pl.multiple_of(col * COLS, COLS), COLS)], cur.at[mine, :], own_sem
    )
    own.start()
    for load in vloads:
        load.wait()

    R = 64

    def prepare_c(i, _):
        first = pl.multiple_of(i * R, R)
        hi, lo = split(masked(c, LAST, TAIL + first, R))
        ch[pl.ds(first, R), :] = hi
        cl[pl.ds(first, R), :] = lo
        return 0

    lax.fori_loop(0, PANEL // R, prepare_c, 0)

    def prepare(i, _):
        first = pl.multiple_of(i * R, R)
        rows = pl.ds(first, R)
        hi, lo = split(masked(pa, off_a, first, R))
        vh[0, rows, :] = hi
        vl[0, rows, :] = lo
        qh[rows, :] = hi
        ql[rows, :] = lo
        hi, lo = split(masked(pb, off_b, first, R))
        vh[1, rows, :] = hi
        vl[1, rows, :] = lo
        return 0

    lax.fori_loop(0, ROWS // R, prepare, 0)

    tload.wait()

    def prepare_t(i, _):
        rows = pl.ds(pl.multiple_of(i * R, R), R)
        for s, panel in ((0, pa), (1, pb), (2, c)):
            hi, lo = split(t3[panel, rows, :])
            th[s, rows, :] = hi
            tl[s, rows, :] = lo
        return 0

    pl.semaphore_wait(barrier, len(greet))
    a2a = []
    for n, (a, b) in enumerate(XY):
        to = in_plane(a, b)
        src = xv.at[:, pl.ds(pl.multiple_of(to[1] * COLS, COLS), COLS)]
        a2a.append(remote(src, cur.at[mine, :], a2a_s.at[n], a2a_r.at[n], to))
    for d in (4, -4):
        pl.semaphore_signal(far0, inc=1, device_id=along_z(d), device_id_type=MESH)

    lax.fori_loop(0, PANEL // R, prepare_t, 0)

    M = 128

    def project(i, _):
        rows = pl.ds(pl.multiple_of(i * M, M), M)
        hi, lo = split(three(mm, ch[rows, :], cl[rows, :], th[2], tl[2]))
        hi, lo = split(three(mm_nt, hi, lo, ch[...], cl[...]))
        ph[rows, :] = hi
        pl_[rows, :] = lo
        return 0

    lax.fori_loop(0, PANEL // M, project, 0)
    tail = pl.ds(TAIL, PANEL)

    def through(i, _):
        rows = pl.ds(pl.multiple_of(i * M, M), M)
        there = pl.ds(pl.multiple_of(TAIL + i * M, M), M)
        moved = three(mm, ph[rows, :], pl_[rows, :], vh[0, tail, :], vl[0, tail, :])
        value = masked(pa, off_a, TAIL + i * M, M)
        hi, lo = split(jnp.where(c == 1, value - moved, value))
        qh[there, :] = hi
        ql[there, :] = lo
        return 0

    lax.fori_loop(0, PANEL // M, through, 0)

    gi, gj = x, y
    bi = pl.ds(pl.multiple_of(gi * 128, 128), 128)
    bj = pl.ds(pl.multiple_of(gj * 128, 128), 128)
    gpart[...] = three(mm_tn, vh[1, :, bi], vl[1, :, bi], qh[:, bj], ql[:, bj])
    gp = remote(gpart.at[pl.ds(pl.multiple_of(other * 64, 64), 64), :], gpair, gp_s, gp_r, partner)

    pl.semaphore_wait(far0, 2)
    for d in (8, -8):
        pl.semaphore_signal(far1, inc=1, device_id=along_z(d), device_id_type=MESH)

    gp.wait()
    gsum[...] = gpart[pl.ds(pl.multiple_of(core * 64, 64), 64), :] + gpair[...]
    slot = lax.rem(z, 8)

    def slot_of(d):
        return lax.rem(z + (d + NZ), 8)

    g_rs = []
    for n, d in enumerate(NEAR):
        src = gsum.at[pl.ds(pl.multiple_of(slot_of(d) * GCHUNK, GCHUNK), GCHUNK), :]
        g_rs.append(remote(src, grs.at[n], grs_s.at[n], grs_r.at[n], along_z(d)))

    own.wait()
    for copy in a2a:
        copy.wait()
    plain = cur[tail, :]
    xh, xl = split(plain)
    moved = plain - three(mm, ph[...], pl_[...], xh, xl)
    for_a = jnp.where(c == 0, moved, plain)
    for_b = jnp.where(c <= 1, moved, plain)
    cur[tail, :] = for_a

    def put(p, cols, value):
        hi, lo = split(value)
        xs[p, pl.ds(0, COLS), cols] = hi
        xs[p, pl.ds(COLS, COLS), cols] = lo

    first = cur[pl.ds(0, TAIL), :].T
    for p, last in ((0, for_a), (1, for_b)):
        put(p, pl.ds(0, TAIL), first)
        put(p, tail, last.T)

    def inner(p):
        both = mm(xs[p], vh[p])
        w2[p] = both[:COLS] + both[COLS:] + mm(xs[p, pl.ds(0, COLS), :], vl[p])

    halves = (0, 1)

    def half(h):
        return pl.ds(h * HALF, HALF)

    def spot(h, s):
        return pl.ds(pl.multiple_of(h * HALF + s * CHUNK, CHUNK), CHUNK)

    inner(other)
    w_p = [remote(w2.at[other, half(h), :], wpair.at[half(h), :], wp_s.at[h], wp_r.at[h], partner) for h in halves]
    inner(core)
    w_rs = []
    for h in halves:
        w_p[h].wait()
        wsum[half(h), :] = w2[core, half(h), :] + wpair[half(h), :]
        w_rs.append([
            remote(wsum.at[spot(h, slot_of(d)), :], wrs.at[h, n], wrs_s.at[h, n], wrs_r.at[h, n], along_z(d))
            for n, d in enumerate(NEAR)
        ])

    for copy in g_rs:
        copy.wait()
    total = gsum[pl.ds(pl.multiple_of(slot * GCHUNK, GCHUNK), GCHUNK), :]
    for n in range(len(NEAR)):
        total = total + grs[n]
    gmine[...] = total
    pl.semaphore_wait(far1, 2)
    g_x = [remote(gmine, gx.at[n], gx_s.at[n], gx_r.at[n], along_z(d)) for n, d in enumerate(FAR)]

    w_x = []
    for h in halves:
        for copy in w_rs[h]:
            copy.wait()
        total = wsum[spot(h, slot), :]
        for n in range(len(NEAR)):
            total = total + wrs[h, n]
        wmine[h] = total
        w_x.append([
            remote(wmine.at[h], wx.at[h, n], wx_s.at[h, n], wx_r.at[h, n], along_z(d))
            for n, d in enumerate(FAR)
        ])

    for copy in g_x:
        copy.wait()
    ghalf = gi * 128 + core * 64
    gspot = (pl.ds(pl.multiple_of(ghalf + slot * GCHUNK, GCHUNK), GCHUNK), bj)
    gfull[gspot] = (gmine[...] + gx[0]) + (gx[1] + gx[2])
    g_ag = [
        remote(gfull.at[gspot], gfull.at[gspot], gag_s.at[n], gag_r.at[n], along_z(d))
        for n, d in enumerate(NEAR)
    ]
    for copy in g_ag:
        copy.wait()
    gown = gfull.at[pl.ds(pl.multiple_of(ghalf, 64), 64), bj]
    g_xy = [remote(gown, gown, gxy_s.at[n], gxy_r.at[n], in_plane(a, b)) for n, (a, b) in enumerate(XY)]

    w_ag = []
    for h in halves:
        for copy in w_x[h]:
            copy.wait()
        at = wfull.at[core, spot(h, slot), :]
        wfull[core, spot(h, slot), :] = (wmine[h] + wx[h, 0]) + (wx[h, 1] + wx[h, 2])
        w_ag.append([
            remote(at, at, wag_s.at[h, n], wag_r.at[h, n], along_z(d)) for n, d in enumerate(NEAR)
        ])
    w_c = []

    def hand_over(h):
        for copy in w_ag[h]:
            copy.wait()
        at = wfull.at[core, half(h), :]
        w_c.append(remote(at, at, wc_s.at[h], wc_r.at[h], partner))

    hand_over(0)
    for copy in g_xy:
        copy.wait()
    g_c = []
    for i in range(4):
        part = gfull.at[pl.ds(pl.multiple_of(i * 128 + core * 64, 64), 64), :]
        g_c.append(remote(part, part, gc_s.at[i], gc_r.at[i], partner))
    hand_over(1)
    for copy in w_c + g_c:
        copy.wait()

    hi, lo = split(wfull[0])
    sa = three(mm_nt, hi, lo, th[0], tl[0])
    sah, sal = split(sa)
    gh, gl = split(gfull[...])
    rest = wfull[1] - three(mm_nt, sah, sal, gh, gl)
    hi, lo = split(rest)
    sb = three(mm_nt, hi, lo, th[1], tl[1])
    sbh, sbl = split(sb)

    def update(p, value, sh, sl):
        both = mm_nt(vh[p], jnp.concatenate([sh, sl], axis=0))
        return value - (both[:, :COLS] + both[:, COLS:] + mm_nt(vl[p], sh))

    after_a = update(0, cur[...], sah, sal)
    cur[...] = after_a
    out_ref[...] = update(1, after_a, sbh, sbl)
    through_c = jnp.where(c == 1, cur[tail, :], out_ref[tail, :])
    xh, xl = split(through_c)
    moved = three(mm, ph[...], pl_[...], xh, xl)
    out_ref[tail, :] = jnp.where(c == 0, out_ref[tail, :], out_ref[tail, :] - moved)


def per_device(eigvecs, reflectors, t_factor, offsets):
    dma = pltpu.SemaphoreType.DMA
    near, far, plane = len(NEAR), len(FAR), len(XY)
    hbm, vmem = pl.BlockSpec(memory_space=pl.ANY), pltpu.VMEM
    return pl.pallas_call(
        kernel,
        out_shape=jax.ShapeDtypeStruct((ROWS, COLS), F32),
        in_specs=[pl.BlockSpec(memory_space=pltpu.SMEM), hbm, hbm, hbm],
        out_specs=pl.BlockSpec(memory_space=pltpu.VMEM),
        scratch_shapes=[
            vmem((PIECE, COLS * NX * NY), F32),
            vmem((ROWS, COLS), F32),
            vmem((3, ROWS, PANEL), F32),
            vmem((3, PANEL, PANEL), F32),
            vmem((2, ROWS, PANEL), BF16),
            vmem((2, ROWS, PANEL), BF16),
            vmem((ROWS, PANEL), BF16),
            vmem((ROWS, PANEL), BF16),
            vmem((PANEL, PANEL), BF16),
            vmem((PANEL, PANEL), BF16),
            vmem((3, PANEL, PANEL), BF16),
            vmem((3, PANEL, PANEL), BF16),
            vmem((PANEL, PANEL), BF16),
            vmem((PANEL, PANEL), BF16),
            vmem((2, 2 * COLS, ROWS), BF16),
            vmem((2, COLS, PANEL), F32),
            vmem((COLS, PANEL), F32),
            vmem((COLS, PANEL), F32),
            vmem((2, near, CHUNK, PANEL), F32),
            vmem((2, far, CHUNK, PANEL), F32),
            vmem((2, CHUNK, PANEL), F32),
            vmem((2, COLS, PANEL), F32),
            vmem((128, 128), F32),
            vmem((64, 128), F32),
            vmem((64, 128), F32),
            vmem((near, GCHUNK, 128), F32),
            vmem((far, GCHUNK, 128), F32),
            vmem((GCHUNK, 128), F32),
            vmem((PANEL, PANEL), F32),
            dma((5,)), dma, dma((plane,)), dma((plane,)), dma, dma, dma((2,)), dma((2,)),
            dma((near,)), dma((near,)), dma((2, near)), dma((2, near)),
            dma((far,)), dma((far,)), dma((2, far)), dma((2, far)),
            dma((near,)), dma((near,)), dma((2, near)), dma((2, near)),
            dma((plane,)), dma((plane,)), dma((4,)), dma((4,)), dma((2,)), dma((2,)),
            pltpu.SemaphoreType.REGULAR, pltpu.SemaphoreType.REGULAR,
        ],
        compiler_params=pltpu.CompilerParams(
            collective_id=0, has_side_effects=True, vmem_limit_bytes=60 * 2**20
        ),
        cost_estimate=pl.CostEstimate(flops=3 * 10**9, bytes_accessed=9 * 10**6, transcendentals=0),
        name="panels",
    )(offsets, eigvecs, reflectors, t_factor)


def solution(mesh):
    return jax.shard_map(
        per_device,
        mesh=mesh,
        in_specs=(P(("row", "col"), None), P(None, "row", None), P(), P()),
        out_specs=P("row", "col"),
        check_vma=False,
    )
```

```python
import jax
import jax.numpy as jnp
from jax import lax
from jax.experimental import pallas as pl
from jax.experimental.pallas import tpu as pltpu
from jax.sharding import PartitionSpec as P

MESH = pl.DeviceIdType.MESH
F32 = jnp.float32
BF16 = jnp.bfloat16

NX, NY, NZ = 4, 4, 32
ROWS, PANEL, COLS = 768, 512, 128
PIECE = 48
TAIL = ROWS - PANEL
LAST = 64 * ROWS - PANEL
NEAR = (4, 3, -3, 2, -2, 1, -1)
FAR = (16, 8, -8)
XY = tuple((a, b) for a in range(NX) for b in range(NY) if (a, b) != (0, 0))
HALF = COLS // 2
CHUNK = HALF // 8
GCHUNK = 8


def split(value):
    hi = value.astype(BF16)
    return hi, (value - hi.astype(F32)).astype(BF16)


def mm(a, b):
    return lax.dot_general(a, b, (((1,), (0,)), ((), ())), preferred_element_type=F32)


def mm_nt(a, b):
    return lax.dot_general(a, b, (((1,), (1,)), ((), ())), preferred_element_type=F32)


def mm_tn(a, b):
    return lax.dot_general(a, b, (((0,), (0,)), ((), ())), preferred_element_type=F32)


def three(dot, ah, al, bh, bl):
    return dot(ah, bh) + (dot(ah, bl) + dot(al, bh))


def kernel(
    off_ref, x_hbm, v_hbm, t_hbm, out_ref,
    xv, cur, v3, t3, vh, vl, ch, cl, th, tl, ph, pl_, xs, w2, wpair, wsum, wrs, wx, wmine, wfull,
    gpart, gpair, gsum, grs, gx, gmine, gfull,
    load_sem, own_sem, a2a_s, a2a_r, gp_s, gp_r, wp_s, wp_r, grs_s, grs_r, wrs_s, wrs_r,
    gx_s, gx_r, wx_s, wx_r, gag_s, gag_r, wag_s, wag_r, gxy_s, gxy_r, gc_s, gc_r, wc_s, wc_r, far0, far1,
):
    row, col = lax.axis_index("row"), lax.axis_index("col")
    z, core = row // 2, lax.rem(row, 2)
    x, y = col // NY, lax.rem(col, NY)
    other = 1 - core

    def along_z(d):
        return (lax.rem(z + (d + NZ), NZ) * 2 + core, col)

    def in_plane(a, b):
        return (row, lax.rem(x + a, NX) * NY + lax.rem(y + b, NY))

    partner = (z * 2 + other, col)

    def remote(src, dst, ssem, rsem, to):
        copy = pltpu.make_async_remote_copy(
            src_ref=src, dst_ref=dst, send_sem=ssem, recv_sem=rsem, device_id=to, device_id_type=MESH
        )
        copy.start()
        return copy

    barrier = pltpu.get_barrier_semaphore()
    greet = [in_plane(a, b) for a, b in XY] + [along_z(d) for d in (4, -4, 3, -3, 2, -2, 1, -1)] + [partner]
    for to in greet:
        pl.semaphore_signal(barrier, inc=1, device_id=to, device_id_type=MESH)

    xload = pltpu.make_async_copy(x_hbm, xv, load_sem.at[0])
    xload.start()
    vloads = [pltpu.make_async_copy(v_hbm.at[p], v3.at[p], load_sem.at[1 + p]) for p in range(3)]
    tload = pltpu.make_async_copy(t_hbm, t3, load_sem.at[4])
    for load in vloads + [tload]:
        load.start()

    c = jnp.where(off_ref[0] == LAST, 0, jnp.where(off_ref[1] == LAST, 1, 2))
    pa = jnp.where(c == 0, 1, 0)
    pb = jnp.where(c == 2, 1, 2)
    off_a, off_b = off_ref[pa], off_ref[pb]

    def masked(panel, start, first, count):
        value = v3[panel, pl.ds(first, count), :]
        step = (
            row * ROWS + first - start
            + lax.broadcasted_iota(jnp.int32, (count, PANEL), 0)
            - lax.broadcasted_iota(jnp.int32, (count, PANEL), 1)
        )
        return jnp.where(step > 0, value, jnp.where(step == 0, F32(1.0), F32(0.0)))

    mine = pl.ds(pl.multiple_of(col * PIECE, PIECE), PIECE)
    xload.wait()
    own = pltpu.make_async_copy(
        xv.at[:, pl.ds(pl.multiple_of(col * COLS, COLS), COLS)], cur.at[mine, :], own_sem
    )
    own.start()
    for load in vloads:
        load.wait()

    R = 64

    def prepare(s, panel, start):
        def some(i, _):
            first = pl.multiple_of(i * R, R)
            hi, lo = split(masked(panel, start, first, R))
            vh[s, pl.ds(first, R), :] = hi
            vl[s, pl.ds(first, R), :] = lo
            return 0

        lax.fori_loop(0, ROWS // R, some, 0)

    prepare(0, pa, off_a)
    pl.semaphore_wait(barrier, len(greet))
    a2a = []
    for n, (a, b) in enumerate(XY):
        to = in_plane(a, b)
        src = xv.at[:, pl.ds(pl.multiple_of(to[1] * COLS, COLS), COLS)]
        a2a.append(remote(src, cur.at[mine, :], a2a_s.at[n], a2a_r.at[n], to))
    for d in (4, -4):
        pl.semaphore_signal(far0, inc=1, device_id=along_z(d), device_id_type=MESH)

    prepare(1, pb, off_b)
    tload.wait()
    tail = pl.ds(TAIL, PANEL)
    end = jnp.where(row == 2 * NZ - 1, 1, 0)
    M = 128

    @pl.when(row == 2 * NZ - 1)
    def _():
        def prepare_c(i, _):
            first = pl.multiple_of(i * R, R)
            rows = pl.ds(first, R)
            hi, lo = split(masked(c, LAST, TAIL + first, R))
            ch[rows, :] = hi
            cl[rows, :] = lo
            hi, lo = split(t3[c, rows, :])
            th[2, rows, :] = hi
            tl[2, rows, :] = lo
            return 0

        lax.fori_loop(0, PANEL // R, prepare_c, 0)

        def project(i, _):
            rows = pl.ds(pl.multiple_of(i * M, M), M)
            hi, lo = split(three(mm, ch[rows, :], cl[rows, :], th[2], tl[2]))
            hi, lo = split(three(mm_nt, hi, lo, ch[...], cl[...]))
            ph[rows, :] = hi
            pl_[rows, :] = lo
            return 0

        lax.fori_loop(0, PANEL // M, project, 0)
        vh[2, pl.ds(0, TAIL), :] = vh[0, pl.ds(0, TAIL), :]
        vl[2, pl.ds(0, TAIL), :] = vl[0, pl.ds(0, TAIL), :]

        def through(i, _):
            rows = pl.ds(pl.multiple_of(i * M, M), M)
            there = pl.ds(pl.multiple_of(TAIL + i * M, M), M)
            moved = three(mm, ph[rows, :], pl_[rows, :], vh[0, tail, :], vl[0, tail, :])
            value = masked(pa, off_a, TAIL + i * M, M)
            hi, lo = split(jnp.where(c == 1, value - moved, value))
            vh[2, there, :] = hi
            vl[2, there, :] = lo
            return 0

        lax.fori_loop(0, PANEL // M, through, 0)

    gi, gj = x, y
    bi = pl.ds(pl.multiple_of(gi * 128, 128), 128)
    bj = pl.ds(pl.multiple_of(gj * 128, 128), 128)
    gpart[...] = three(mm_tn, vh[1, :, bi], vl[1, :, bi], vh[2 * end, :, bj], vl[2 * end, :, bj])
    gp = remote(gpart.at[pl.ds(pl.multiple_of(other * 64, 64), 64), :], gpair, gp_s, gp_r, partner)

    pl.semaphore_wait(far0, 2)
    for d in (8, -8):
        pl.semaphore_signal(far1, inc=1, device_id=along_z(d), device_id_type=MESH)

    gp.wait()
    gsum[...] = gpart[pl.ds(pl.multiple_of(core * 64, 64), 64), :] + gpair[...]
    slot = lax.rem(z, 8)

    def slot_of(d):
        return lax.rem(z + (d + NZ), 8)

    g_rs = []
    for n, d in enumerate(NEAR):
        src = gsum.at[pl.ds(pl.multiple_of(slot_of(d) * GCHUNK, GCHUNK), GCHUNK), :]
        g_rs.append(remote(src, grs.at[n], grs_s.at[n], grs_r.at[n], along_z(d)))

    own.wait()
    for copy in a2a:
        copy.wait()
    def put(p, cols, value):
        hi, lo = split(value)
        xs[p, pl.ds(0, COLS), cols] = hi
        xs[p, pl.ds(COLS, COLS), cols] = lo

    @pl.when(row == 2 * NZ - 1)
    def _():
        plain = cur[tail, :]
        xh, xl = split(plain)
        moved = plain - three(mm, ph[...], pl_[...], xh, xl)
        cur[tail, :] = jnp.where(c == 0, moved, plain)
        put(1, pl.ds(0, TAIL), cur[pl.ds(0, TAIL), :].T)
        put(1, tail, jnp.where(c <= 1, moved, plain).T)

    put(0, pl.ds(0, ROWS), cur[...].T)

    def inner(p):
        value = xs.at[p * end]
        both = mm(value[...], vh[p])
        w2[p] = both[:COLS] + both[COLS:] + mm(value[pl.ds(0, COLS), :], vl[p])

    halves = (0, 1)

    def half(h):
        return pl.ds(h * HALF, HALF)

    def spot(h, s):
        return pl.ds(pl.multiple_of(h * HALF + s * CHUNK, CHUNK), CHUNK)

    inner(other)
    w_p = [remote(w2.at[other, half(h), :], wpair.at[half(h), :], wp_s.at[h], wp_r.at[h], partner) for h in halves]
    inner(core)
    w_rs = []
    for h in halves:
        w_p[h].wait()
        wsum[half(h), :] = w2[core, half(h), :] + wpair[half(h), :]
        w_rs.append([
            remote(wsum.at[spot(h, slot_of(d)), :], wrs.at[h, n], wrs_s.at[h, n], wrs_r.at[h, n], along_z(d))
            for n, d in enumerate(NEAR)
        ])

    for copy in g_rs:
        copy.wait()
    total = gsum[pl.ds(pl.multiple_of(slot * GCHUNK, GCHUNK), GCHUNK), :]
    for n in range(len(NEAR)):
        total = total + grs[n]
    gmine[...] = total
    pl.semaphore_wait(far1, 2)
    g_x = [remote(gmine, gx.at[n], gx_s.at[n], gx_r.at[n], along_z(d)) for n, d in enumerate(FAR)]

    def prepare_t(i, _):
        rows = pl.ds(pl.multiple_of(i * R, R), R)
        for s, panel in ((0, pa), (1, pb)):
            hi, lo = split(t3[panel, rows, :])
            th[s, rows, :] = hi
            tl[s, rows, :] = lo
        return 0

    lax.fori_loop(0, PANEL // R, prepare_t, 0)
    w_x = []
    for h in halves:
        for copy in w_rs[h]:
            copy.wait()
        total = wsum[spot(h, slot), :]
        for n in range(len(NEAR)):
            total = total + wrs[h, n]
        wmine[h] = total
        w_x.append([
            remote(wmine.at[h], wx.at[h, n], wx_s.at[h, n], wx_r.at[h, n], along_z(d))
            for n, d in enumerate(FAR)
        ])

    for copy in g_x:
        copy.wait()
    ghalf = gi * 128 + core * 64
    gspot = (pl.ds(pl.multiple_of(ghalf + slot * GCHUNK, GCHUNK), GCHUNK), bj)
    gfull[gspot] = (gmine[...] + gx[0]) + (gx[1] + gx[2])
    g_ag = [
        remote(gfull.at[gspot], gfull.at[gspot], gag_s.at[n], gag_r.at[n], along_z(d))
        for n, d in enumerate(NEAR)
    ]
    for copy in g_ag:
        copy.wait()
    gown = gfull.at[pl.ds(pl.multiple_of(ghalf, 64), 64), bj]
    g_xy = [remote(gown, gown, gxy_s.at[n], gxy_r.at[n], in_plane(a, b)) for n, (a, b) in enumerate(XY)]

    w_ag = []
    for h in halves:
        for copy in w_x[h]:
            copy.wait()
        at = wfull.at[core, spot(h, slot), :]
        wfull[core, spot(h, slot), :] = (wmine[h] + wx[h, 0]) + (wx[h, 1] + wx[h, 2])
        w_ag.append([
            remote(at, at, wag_s.at[h, n], wag_r.at[h, n], along_z(d)) for n, d in enumerate(NEAR)
        ])
    w_c = []

    def hand_over(h):
        for copy in w_ag[h]:
            copy.wait()
        at = wfull.at[core, half(h), :]
        w_c.append(remote(at, at, wc_s.at[h], wc_r.at[h], partner))

    hand_over(0)
    for copy in g_xy:
        copy.wait()
    g_c = []
    for i in range(4):
        part = gfull.at[pl.ds(pl.multiple_of(i * 128 + core * 64, 64), 64), :]
        g_c.append(remote(part, part, gc_s.at[i], gc_r.at[i], partner))
    hand_over(1)
    for copy in w_c + g_c:
        copy.wait()

    hi, lo = split(wfull[0])
    sa = three(mm_nt, hi, lo, th[0], tl[0])
    sah, sal = split(sa)
    gh, gl = split(gfull[...])
    rest = wfull[1] - three(mm_nt, sah, sal, gh, gl)
    hi, lo = split(rest)
    sb = three(mm_nt, hi, lo, th[1], tl[1])
    sbh, sbl = split(sb)

    def update(p, value, sh, sl):
        both = mm_nt(vh[p], jnp.concatenate([sh, sl], axis=0))
        return value - (both[:, :COLS] + both[:, COLS:] + mm_nt(vl[p], sh))

    after_a = update(0, cur[...], sah, sal)
    cur[...] = after_a
    out_ref[...] = update(1, after_a, sbh, sbl)

    @pl.when(row == 2 * NZ - 1)
    def _():
        after_b = out_ref[tail, :]
        xh, xl = split(jnp.where(c == 1, cur[tail, :], after_b))
        moved = three(mm, ph[...], pl_[...], xh, xl)
        out_ref[tail, :] = jnp.where(c == 0, after_b, after_b - moved)


def per_device(eigvecs, reflectors, t_factor, offsets):
    dma = pltpu.SemaphoreType.DMA
    near, far, plane = len(NEAR), len(FAR), len(XY)
    hbm, vmem = pl.BlockSpec(memory_space=pl.ANY), pltpu.VMEM
    return pl.pallas_call(
        kernel,
        out_shape=jax.ShapeDtypeStruct((ROWS, COLS), F32),
        in_specs=[pl.BlockSpec(memory_space=pltpu.SMEM), hbm, hbm, hbm],
        out_specs=pl.BlockSpec(memory_space=pltpu.VMEM),
        scratch_shapes=[
            vmem((PIECE, COLS * NX * NY), F32),
            vmem((ROWS, COLS), F32),
            vmem((3, ROWS, PANEL), F32),
            vmem((3, PANEL, PANEL), F32),
            vmem((3, ROWS, PANEL), BF16),
            vmem((3, ROWS, PANEL), BF16),
            vmem((PANEL, PANEL), BF16),
            vmem((PANEL, PANEL), BF16),
            vmem((3, PANEL, PANEL), BF16),
            vmem((3, PANEL, PANEL), BF16),
            vmem((PANEL, PANEL), BF16),
            vmem((PANEL, PANEL), BF16),
            vmem((2, 2 * COLS, ROWS), BF16),
            vmem((2, COLS, PANEL), F32),
            vmem((COLS, PANEL), F32),
            vmem((COLS, PANEL), F32),
            vmem((2, near, CHUNK, PANEL), F32),
            vmem((2, far, CHUNK, PANEL), F32),
            vmem((2, CHUNK, PANEL), F32),
            vmem((2, COLS, PANEL), F32),
            vmem((128, 128), F32),
            vmem((64, 128), F32),
            vmem((64, 128), F32),
            vmem((near, GCHUNK, 128), F32),
            vmem((far, GCHUNK, 128), F32),
            vmem((GCHUNK, 128), F32),
            vmem((PANEL, PANEL), F32),
            dma((5,)), dma, dma((plane,)), dma((plane,)), dma, dma, dma((2,)), dma((2,)),
            dma((near,)), dma((near,)), dma((2, near)), dma((2, near)),
            dma((far,)), dma((far,)), dma((2, far)), dma((2, far)),
            dma((near,)), dma((near,)), dma((2, near)), dma((2, near)),
            dma((plane,)), dma((plane,)), dma((4,)), dma((4,)), dma((2,)), dma((2,)),
            pltpu.SemaphoreType.REGULAR, pltpu.SemaphoreType.REGULAR,
        ],
        compiler_params=pltpu.CompilerParams(
            collective_id=0, has_side_effects=True, vmem_limit_bytes=54600 * 2**10
        ),
        cost_estimate=pl.CostEstimate(flops=3 * 10**9, bytes_accessed=9 * 10**6, transcendentals=0),
        name="panels",
    )(offsets, eigvecs, reflectors, t_factor)


def solution(mesh):
    return jax.shard_map(
        per_device,
        mesh=mesh,
        in_specs=(P(("row", "col"), None), P(None, "row", None), P(), P()),
        out_specs=P("row", "col"),
        check_vma=False,
    )
```

```python
import jax
import jax.numpy as jnp
from jax import lax
from jax.experimental import pallas as pl
from jax.experimental.pallas import tpu as pltpu
from jax.sharding import PartitionSpec as P

MESH = pl.DeviceIdType.MESH
F32 = jnp.float32
BF16 = jnp.bfloat16

NX, NY, NZ = 4, 4, 32
ROWS, PANEL, COLS = 768, 512, 128
PIECE = 48
TAIL = ROWS - PANEL
LAST = 64 * ROWS - PANEL
NEAR = (4, 3, -3, 2, -2, 1, -1)
FAR = (12, -12, 4, -4)
XY = tuple((a, b) for a in range(NX) for b in range(NY) if (a, b) != (0, 0))
HALF = COLS // 2
CHUNK = HALF // 8
GCHUNK = 8


def split(value):
    hi = value.astype(BF16)
    return hi, (value - hi.astype(F32)).astype(BF16)


def mm(a, b):
    return lax.dot_general(a, b, (((1,), (0,)), ((), ())), preferred_element_type=F32)


def mm_nt(a, b):
    return lax.dot_general(a, b, (((1,), (1,)), ((), ())), preferred_element_type=F32)


def mm_tn(a, b):
    return lax.dot_general(a, b, (((0,), (0,)), ((), ())), preferred_element_type=F32)


def three(dot, ah, al, bh, bl):
    return dot(ah, bh) + (dot(ah, bl) + dot(al, bh))


def kernel(
    off_ref, x_hbm, v_hbm, t_hbm, out_ref,
    xv, cur, v3, t3, vh, vl, ch, cl, th, tl, ph, pl_, xs, sah, sal, w2, wpair, wsum, wrs, wx, wmine, wfull,
    gpart, gpair, gsum, grs, gx, gmine, gfull,
    load_sem, own_sem, a2a_s, a2a_r, gp_s, gp_r, wp_s, wp_r, grs_s, grs_r, wrs_s, wrs_r,
    gx_s, gx_r, wx_s, wx_r, gag_s, gag_r, wag_s, wag_r, gxy_s, gxy_r, gc_s, gc_r, wc_s, wc_r, far0, far1,
):
    row, col = lax.axis_index("row"), lax.axis_index("col")
    z, core = row // 2, lax.rem(row, 2)
    x, y = col // NY, lax.rem(col, NY)
    other = 1 - core
    part = 1 - core

    def along_z(d):
        return (lax.rem(z + (d + NZ), NZ) * 2 + core, col)

    def in_plane(a, b):
        return (row, lax.rem(x + a, NX) * NY + lax.rem(y + b, NY))

    partner = (z * 2 + other, col)

    def remote(src, dst, ssem, rsem, to):
        copy = pltpu.make_async_remote_copy(
            src_ref=src, dst_ref=dst, send_sem=ssem, recv_sem=rsem, device_id=to, device_id_type=MESH
        )
        copy.start()
        return copy

    barrier = pltpu.get_barrier_semaphore()
    greet = [in_plane(a, b) for a, b in XY] + [along_z(d) for d in (4, -4, 3, -3, 2, -2, 1, -1)] + [partner]
    for to in greet:
        pl.semaphore_signal(barrier, inc=1, device_id=to, device_id_type=MESH)

    xload = pltpu.make_async_copy(x_hbm, xv, load_sem.at[0])
    xload.start()
    vloads = [pltpu.make_async_copy(v_hbm.at[p], v3.at[p], load_sem.at[1 + p]) for p in range(3)]
    tload = pltpu.make_async_copy(t_hbm, t3, load_sem.at[4])
    for load in vloads:
        load.start()

    c = jnp.where(off_ref[0] == LAST, 0, jnp.where(off_ref[1] == LAST, 1, 2))
    pa = jnp.where(c == 0, 1, 0)
    pb = jnp.where(c == 2, 1, 2)
    off_a, off_b = off_ref[pa], off_ref[pb]

    def masked(panel, start, first, count):
        value = v3[panel, pl.ds(first, count), :]
        step = (
            row * ROWS + first - start
            + lax.broadcasted_iota(jnp.int32, (count, PANEL), 0)
            - lax.broadcasted_iota(jnp.int32, (count, PANEL), 1)
        )
        return jnp.where(step > 0, value, jnp.where(step == 0, F32(1.0), F32(0.0)))

    mine = pl.ds(pl.multiple_of(col * PIECE, PIECE), PIECE)
    xload.wait()
    own = pltpu.make_async_copy(
        xv.at[:, pl.ds(pl.multiple_of(col * COLS, COLS), COLS)], cur.at[mine, :], own_sem
    )
    own.start()
    pl.semaphore_wait(barrier, len(greet))
    a2a = []
    for n, (a, b) in enumerate(XY):
        to = in_plane(a, b)
        src = xv.at[:, pl.ds(pl.multiple_of(to[1] * COLS, COLS), COLS)]
        a2a.append(remote(src, cur.at[mine, :], a2a_s.at[n], a2a_r.at[n], to))
    for d in (4, -4):
        pl.semaphore_signal(far0, inc=1, device_id=along_z(d), device_id_type=MESH)

    for load in vloads:
        load.wait()
    tload.start()
    R = 64

    def prepare(s, panel, start):
        def some(i, _):
            first = pl.multiple_of(i * R, R)
            hi, lo = split(masked(panel, start, first, R))
            vh[s, pl.ds(first, R), :] = hi
            vl[s, pl.ds(first, R), :] = lo
            return 0

        lax.fori_loop(0, ROWS // R, some, 0)

    prepare(0, pa, off_a)
    prepare(1, pb, off_b)
    pl.semaphore_wait(far0, 2)
    for d in (4, -4):
        pl.semaphore_signal(far1, inc=1, device_id=along_z(d), device_id_type=MESH)
    tload.wait()
    tail = pl.ds(TAIL, PANEL)
    end = jnp.where(row == 2 * NZ - 1, 1, 0)
    M = 128

    @pl.when(row == 2 * NZ - 1)
    def _():
        def prepare_c(i, _):
            first = pl.multiple_of(i * R, R)
            rows = pl.ds(first, R)
            hi, lo = split(masked(c, LAST, TAIL + first, R))
            ch[rows, :] = hi
            cl[rows, :] = lo
            hi, lo = split(t3[c, rows, :])
            th[2, rows, :] = hi
            tl[2, rows, :] = lo
            return 0

        lax.fori_loop(0, PANEL // R, prepare_c, 0)

        def project(i, _):
            rows = pl.ds(pl.multiple_of(i * M, M), M)
            hi, lo = split(three(mm, ch[rows, :], cl[rows, :], th[2], tl[2]))
            hi, lo = split(three(mm_nt, hi, lo, ch[...], cl[...]))
            ph[rows, :] = hi
            pl_[rows, :] = lo
            return 0

        lax.fori_loop(0, PANEL // M, project, 0)
        vh[2, pl.ds(0, TAIL), :] = vh[0, pl.ds(0, TAIL), :]
        vl[2, pl.ds(0, TAIL), :] = vl[0, pl.ds(0, TAIL), :]

        def through(i, _):
            rows = pl.ds(pl.multiple_of(i * M, M), M)
            there = pl.ds(pl.multiple_of(TAIL + i * M, M), M)
            moved = three(mm, ph[rows, :], pl_[rows, :], vh[0, tail, :], vl[0, tail, :])
            value = masked(pa, off_a, TAIL + i * M, M)
            hi, lo = split(jnp.where(c == 1, value - moved, value))
            vh[2, there, :] = hi
            vl[2, there, :] = lo
            return 0

        lax.fori_loop(0, PANEL // M, through, 0)

    gi, gj = x, y
    bi = pl.ds(pl.multiple_of(gi * 128, 128), 128)
    bj = pl.ds(pl.multiple_of(gj * 128, 128), 128)
    gpart[...] = three(mm_tn, vh[1, :, bi], vl[1, :, bi], vh[2 * end, :, bj], vl[2 * end, :, bj])
    gp = remote(gpart.at[pl.ds(pl.multiple_of(other * 64, 64), 64), :], gpair, gp_s, gp_r, partner)

    gp.wait()
    gsum[...] = gpart[pl.ds(pl.multiple_of(core * 64, 64), 64), :] + gpair[...]
    slot = lax.rem(z, 8)
    final = lax.rem(z + 4, 8)

    def slot_of(d):
        return lax.rem(z + (d + NZ), 8)

    g_rs = []
    for n, d in enumerate(NEAR):
        src = gsum.at[pl.ds(pl.multiple_of(slot_of(d) * GCHUNK, GCHUNK), GCHUNK), :]
        g_rs.append(remote(src, grs.at[n], grs_s.at[n], grs_r.at[n], along_z(d)))

    own.wait()
    for copy in a2a:
        copy.wait()
    def put(p, cols, value):
        hi, lo = split(value)
        xs[p, pl.ds(0, COLS), cols] = hi
        xs[p, pl.ds(COLS, COLS), cols] = lo

    @pl.when(row == 2 * NZ - 1)
    def _():
        plain = cur[tail, :]
        xh, xl = split(plain)
        moved = plain - three(mm, ph[...], pl_[...], xh, xl)
        cur[tail, :] = jnp.where(c == 0, moved, plain)
        put(1, pl.ds(0, TAIL), cur[pl.ds(0, TAIL), :].T)
        put(1, tail, jnp.where(c <= 1, moved, plain).T)

    put(0, pl.ds(0, ROWS), cur[...].T)

    def inner(p):
        value = xs.at[p * end]
        both = mm(value[...], vh[p])
        w2[p] = both[:COLS] + both[COLS:] + mm(value[pl.ds(0, COLS), :], vl[p])

    halves = (0, 1)

    def half(h):
        return pl.ds(h * HALF, HALF)

    def spot(h, s):
        return pl.ds(pl.multiple_of(h * HALF + s * CHUNK, CHUNK), CHUNK)

    inner(core)
    w_p = [remote(w2.at[core, half(h), :], wpair.at[half(h), :], wp_s.at[h], wp_r.at[h], partner) for h in halves]
    inner(part)
    w_rs = []
    for h in halves:
        w_p[h].wait()
        wsum[half(h), :] = w2[part, half(h), :] + wpair[half(h), :]
        w_rs.append([
            remote(wsum.at[spot(h, slot_of(d)), :], wrs.at[h, n], wrs_s.at[h, n], wrs_r.at[h, n], along_z(d))
            for n, d in enumerate(NEAR)
        ])

    for copy in g_rs:
        copy.wait()
    total = gsum[pl.ds(pl.multiple_of(slot * GCHUNK, GCHUNK), GCHUNK), :]
    for n in range(len(NEAR)):
        total = total + grs[n]
    gmine[...] = total
    pl.semaphore_wait(far1, 2)
    g_x = [remote(gmine, gx.at[n], gx_s.at[n], gx_r.at[n], along_z(d)) for n, d in enumerate(FAR)]

    def prepare_t(i, _):
        rows = pl.ds(pl.multiple_of(i * R, R), R)
        for s, panel in ((0, pa), (1, pb)):
            hi, lo = split(t3[panel, rows, :])
            th[s, rows, :] = hi
            tl[s, rows, :] = lo
        return 0

    lax.fori_loop(0, PANEL // R, prepare_t, 0)
    w_x = []
    for h in halves:
        for copy in w_rs[h]:
            copy.wait()
        total = wsum[spot(h, slot), :]
        for n in range(len(NEAR)):
            total = total + wrs[h, n]
        wmine[h] = total
        w_x.append([
            remote(wmine.at[h], wx.at[h, n], wx_s.at[h, n], wx_r.at[h, n], along_z(d))
            for n, d in enumerate(FAR)
        ])

    for copy in g_x:
        copy.wait()
    ghalf = gi * 128 + core * 64
    gspot = (pl.ds(pl.multiple_of(ghalf + final * GCHUNK, GCHUNK), GCHUNK), bj)
    gfull[gspot] = (gx[0] + gx[1]) + (gx[2] + gx[3])
    g_ag = [
        remote(gfull.at[gspot], gfull.at[gspot], gag_s.at[n], gag_r.at[n], along_z(d))
        for n, d in enumerate(NEAR)
    ]
    for copy in g_ag:
        copy.wait()
    gown = gfull.at[pl.ds(pl.multiple_of(ghalf, 64), 64), bj]
    g_xy = [remote(gown, gown, gxy_s.at[n], gxy_r.at[n], in_plane(a, b)) for n, (a, b) in enumerate(XY)]

    w_ag = []
    for h in halves:
        for copy in w_x[h]:
            copy.wait()
        at = wfull.at[part, spot(h, final), :]
        wfull[part, spot(h, final), :] = (wx[h, 0] + wx[h, 1]) + (wx[h, 2] + wx[h, 3])
        w_ag.append([
            remote(at, at, wag_s.at[h, n], wag_r.at[h, n], along_z(d)) for n, d in enumerate(NEAR)
        ])
    w_c = []

    def hand_over(h):
        for copy in w_ag[h]:
            copy.wait()
        at = wfull.at[part, half(h), :]
        w_c.append(remote(at, at, wc_s.at[h], wc_r.at[h], partner))

    hand_over(0)
    for copy in g_xy:
        copy.wait()
    g_c = []
    for i in range(4):
        strip = gfull.at[pl.ds(pl.multiple_of(i * 128 + core * 64, 64), 64), :]
        g_c.append(remote(strip, strip, gc_s.at[i], gc_r.at[i], partner))
    hand_over(1)
    def update(p, value, sh, sl):
        both = mm_nt(vh[p], jnp.concatenate([sh, sl], axis=0))
        return value - (both[:, :COLS] + both[:, COLS:] + mm_nt(vl[p], sh))

    def apply_a():
        hi, lo = split(wfull[0])
        hi, lo = split(three(mm_nt, hi, lo, th[0], tl[0]))
        sah[...] = hi
        sal[...] = lo
        cur[...] = update(0, cur[...], hi, lo)

    @pl.when(core == 1)
    def _():
        apply_a()

    for copy in w_c:
        copy.wait()

    @pl.when(core == 0)
    def _():
        apply_a()

    for copy in g_c:
        copy.wait()
    gh, gl = split(gfull[...])
    hi, lo = split(wfull[1] - three(mm_nt, sah[...], sal[...], gh, gl))
    hi, lo = split(three(mm_nt, hi, lo, th[1], tl[1]))
    out_ref[...] = update(1, cur[...], hi, lo)

    @pl.when(row == 2 * NZ - 1)
    def _():
        after_b = out_ref[tail, :]
        xh, xl = split(jnp.where(c == 1, cur[tail, :], after_b))
        moved = three(mm, ph[...], pl_[...], xh, xl)
        out_ref[tail, :] = jnp.where(c == 0, after_b, after_b - moved)


def per_device(eigvecs, reflectors, t_factor, offsets):
    dma = pltpu.SemaphoreType.DMA
    near, far, plane = len(NEAR), len(FAR), len(XY)
    hbm, vmem = pl.BlockSpec(memory_space=pl.ANY), pltpu.VMEM
    return pl.pallas_call(
        kernel,
        out_shape=jax.ShapeDtypeStruct((ROWS, COLS), F32),
        in_specs=[pl.BlockSpec(memory_space=pltpu.SMEM), hbm, hbm, hbm],
        out_specs=pl.BlockSpec(memory_space=pltpu.VMEM),
        scratch_shapes=[
            vmem((PIECE, COLS * NX * NY), F32),
            vmem((ROWS, COLS), F32),
            vmem((3, ROWS, PANEL), F32),
            vmem((3, PANEL, PANEL), F32),
            vmem((3, ROWS, PANEL), BF16),
            vmem((3, ROWS, PANEL), BF16),
            vmem((PANEL, PANEL), BF16),
            vmem((PANEL, PANEL), BF16),
            vmem((3, PANEL, PANEL), BF16),
            vmem((3, PANEL, PANEL), BF16),
            vmem((PANEL, PANEL), BF16),
            vmem((PANEL, PANEL), BF16),
            vmem((2, 2 * COLS, ROWS), BF16),
            vmem((COLS, PANEL), BF16),
            vmem((COLS, PANEL), BF16),
            vmem((2, COLS, PANEL), F32),
            vmem((COLS, PANEL), F32),
            vmem((COLS, PANEL), F32),
            vmem((2, near, CHUNK, PANEL), F32),
            vmem((2, far, CHUNK, PANEL), F32),
            vmem((2, CHUNK, PANEL), F32),
            vmem((2, COLS, PANEL), F32),
            vmem((128, 128), F32),
            vmem((64, 128), F32),
            vmem((64, 128), F32),
            vmem((near, GCHUNK, 128), F32),
            vmem((far, GCHUNK, 128), F32),
            vmem((GCHUNK, 128), F32),
            vmem((PANEL, PANEL), F32),
            dma((5,)), dma, dma((plane,)), dma((plane,)), dma, dma, dma((2,)), dma((2,)),
            dma((near,)), dma((near,)), dma((2, near)), dma((2, near)),
            dma((far,)), dma((far,)), dma((2, far)), dma((2, far)),
            dma((near,)), dma((near,)), dma((2, near)), dma((2, near)),
            dma((plane,)), dma((plane,)), dma((4,)), dma((4,)), dma((2,)), dma((2,)),
            pltpu.SemaphoreType.REGULAR, pltpu.SemaphoreType.REGULAR,
        ],
        compiler_params=pltpu.CompilerParams(
            collective_id=0, has_side_effects=True, vmem_limit_bytes=54600 * 2**10
        ),
        cost_estimate=pl.CostEstimate(flops=3 * 10**9, bytes_accessed=9 * 10**6, transcendentals=0),
        name="panels",
    )(offsets, eigvecs, reflectors, t_factor)


def solution(mesh):
    return jax.shard_map(
        per_device,
        mesh=mesh,
        in_specs=(P(("row", "col"), None), P(None, "row", None), P(), P()),
        out_specs=P("row", "col"),
        check_vma=False,
    )
```

```python
import jax
import jax.numpy as jnp
from jax import lax
from jax.experimental import pallas as pl
from jax.experimental.pallas import tpu as pltpu
from jax.sharding import PartitionSpec as P

MESH = pl.DeviceIdType.MESH
F32 = jnp.float32
BF16 = jnp.bfloat16

NX, NY, NZ = 4, 4, 32
ROWS, PANEL, COLS = 768, 512, 128
PIECE = 48
TAIL = ROWS - PANEL
LAST = 64 * ROWS - PANEL
NEAR = (4, 3, -3, 2, -2, 1, -1)
FAR = (12, -12, 4, -4)
XY = tuple((a, b) for a in range(NX) for b in range(NY) if (a, b) != (0, 0))
HALF = COLS // 2
CHUNK = HALF // 8
GCHUNK = 8


def split(value):
    hi = value.astype(BF16)
    return hi, (value - hi.astype(F32)).astype(BF16)


def mm(a, b):
    return lax.dot_general(a, b, (((1,), (0,)), ((), ())), preferred_element_type=F32)


def mm_nt(a, b):
    return lax.dot_general(a, b, (((1,), (1,)), ((), ())), preferred_element_type=F32)


def mm_tn(a, b):
    return lax.dot_general(a, b, (((0,), (0,)), ((), ())), preferred_element_type=F32)


def three(dot, ah, al, bh, bl):
    return dot(ah, bh) + (dot(ah, bl) + dot(al, bh))


def kernel(
    off_ref, x_hbm, v_hbm, t_hbm, out_ref,
    xv, cur, v3, t3, vh, vl, ch, cl, th, tl, ph, pl_, xs, sah, sal, w2, wpair, wsum, wrs, wx, wmine, wfull,
    gpart, gpair, gsum, grs, gx, gmine, gfull,
    load_sem, own_sem, a2a_s, a2a_r, gp_s, gp_r, wp_s, wp_r, grs_s, grs_r, wrs_s, wrs_r,
    gx_s, gx_r, wx_s, wx_r, gag_s, gag_r, wag_s, wag_r, gxy_s, gxy_r, gc_s, gc_r, wc_s, wc_r, far0, far1,
):
    row, col = lax.axis_index("row"), lax.axis_index("col")
    z, core = row // 2, lax.rem(row, 2)
    x, y = col // NY, lax.rem(col, NY)
    other = 1 - core
    part = 1 - core

    def along_z(d):
        return (lax.rem(z + (d + NZ), NZ) * 2 + core, col)

    def in_plane(a, b):
        return (row, lax.rem(x + a, NX) * NY + lax.rem(y + b, NY))

    partner = (z * 2 + other, col)

    def remote(src, dst, ssem, rsem, to):
        copy = pltpu.make_async_remote_copy(
            src_ref=src, dst_ref=dst, send_sem=ssem, recv_sem=rsem, device_id=to, device_id_type=MESH
        )
        copy.start()
        return copy

    barrier = pltpu.get_barrier_semaphore()
    greet = [in_plane(a, b) for a, b in XY] + [along_z(d) for d in (4, -4, 3, -3, 2, -2, 1, -1)] + [partner]
    for to in greet:
        pl.semaphore_signal(barrier, inc=1, device_id=to, device_id_type=MESH)

    xload = pltpu.make_async_copy(x_hbm, xv, load_sem.at[0])
    xload.start()
    vloads = [pltpu.make_async_copy(v_hbm.at[p], v3.at[p], load_sem.at[1 + p]) for p in range(3)]
    tload = pltpu.make_async_copy(t_hbm, t3, load_sem.at[4])
    for load in vloads:
        load.start()

    c = jnp.where(off_ref[0] == LAST, 0, jnp.where(off_ref[1] == LAST, 1, 2))
    pa = jnp.where(c == 0, 1, 0)
    pb = jnp.where(c == 2, 1, 2)
    off_a, off_b = off_ref[pa], off_ref[pb]

    def masked(panel, start, first, count):
        value = v3[panel, pl.ds(first, count), :]
        step = (
            row * ROWS + first - start
            + lax.broadcasted_iota(jnp.int32, (count, PANEL), 0)
            - lax.broadcasted_iota(jnp.int32, (count, PANEL), 1)
        )
        return jnp.where(step > 0, value, jnp.where(step == 0, F32(1.0), F32(0.0)))

    mine = pl.ds(pl.multiple_of(col * PIECE, PIECE), PIECE)
    xload.wait()
    own = pltpu.make_async_copy(
        xv.at[:, pl.ds(pl.multiple_of(col * COLS, COLS), COLS)], cur.at[mine, :], own_sem
    )
    own.start()
    pl.semaphore_wait(barrier, len(greet))
    a2a = []
    for n, (a, b) in enumerate(XY):
        to = in_plane(a, b)
        src = xv.at[:, pl.ds(pl.multiple_of(to[1] * COLS, COLS), COLS)]
        a2a.append(remote(src, cur.at[mine, :], a2a_s.at[n], a2a_r.at[n], to))
    for d in (4, -4):
        pl.semaphore_signal(far0, inc=1, device_id=along_z(d), device_id_type=MESH)

    for load in vloads:
        load.wait()
    tload.start()
    R = 64

    def prepare(s, panel, start):
        def some(i, _):
            first = pl.multiple_of(i * R, R)
            hi, lo = split(masked(panel, start, first, R))
            vh[s, pl.ds(first, R), :] = hi
            vl[s, pl.ds(first, R), :] = lo
            return 0

        lax.fori_loop(0, ROWS // R, some, 0)

    prepare(0, pa, off_a)
    prepare(1, pb, off_b)
    pl.semaphore_wait(far0, 2)
    for d in (4, -4):
        pl.semaphore_signal(far1, inc=1, device_id=along_z(d), device_id_type=MESH)
    tload.wait()
    tail = pl.ds(TAIL, PANEL)
    end = jnp.where(row == 2 * NZ - 1, 1, 0)
    M = 128

    @pl.when(row == 2 * NZ - 1)
    def _():
        def prepare_c(i, _):
            first = pl.multiple_of(i * R, R)
            rows = pl.ds(first, R)
            hi, lo = split(masked(c, LAST, TAIL + first, R))
            ch[rows, :] = hi
            cl[rows, :] = lo
            hi, lo = split(t3[c, rows, :])
            th[2, rows, :] = hi
            tl[2, rows, :] = lo
            return 0

        lax.fori_loop(0, PANEL // R, prepare_c, 0)

        def project(i, _):
            rows = pl.ds(pl.multiple_of(i * M, M), M)
            hi, lo = split(three(mm, ch[rows, :], cl[rows, :], th[2], tl[2]))
            hi, lo = split(three(mm_nt, hi, lo, ch[...], cl[...]))
            ph[rows, :] = hi
            pl_[rows, :] = lo
            return 0

        lax.fori_loop(0, PANEL // M, project, 0)
        vh[2, pl.ds(0, TAIL), :] = vh[0, pl.ds(0, TAIL), :]
        vl[2, pl.ds(0, TAIL), :] = vl[0, pl.ds(0, TAIL), :]

        def through(i, _):
            rows = pl.ds(pl.multiple_of(i * M, M), M)
            there = pl.ds(pl.multiple_of(TAIL + i * M, M), M)
            moved = three(mm, ph[rows, :], pl_[rows, :], vh[0, tail, :], vl[0, tail, :])
            value = masked(pa, off_a, TAIL + i * M, M)
            hi, lo = split(jnp.where(c == 1, value - moved, value))
            vh[2, there, :] = hi
            vl[2, there, :] = lo
            return 0

        lax.fori_loop(0, PANEL // M, through, 0)

    gi, gj = x, y
    bi = pl.ds(pl.multiple_of(gi * 128, 128), 128)
    bj = pl.ds(pl.multiple_of(gj * 128, 128), 128)
    gpart[...] = three(mm_tn, vh[1, :, bi], vl[1, :, bi], vh[2 * end, :, bj], vl[2 * end, :, bj])
    gp = remote(gpart.at[pl.ds(pl.multiple_of(other * 64, 64), 64), :], gpair, gp_s, gp_r, partner)

    gp.wait()
    gsum[...] = gpart[pl.ds(pl.multiple_of(core * 64, 64), 64), :] + gpair[...]
    slot = lax.rem(z, 8)
    final = lax.rem(z + 4, 8)

    def near(h):
        sign = 1 - 2 * lax.rem(core + h, 2)
        return [(n, d * sign) for n, d in enumerate(NEAR)]

    def slot_of(d):
        return lax.rem(z + (d + NZ), 8)

    g_rs = []
    for n, d in near(0):
        src = gsum.at[pl.ds(pl.multiple_of(slot_of(d) * GCHUNK, GCHUNK), GCHUNK), :]
        g_rs.append(remote(src, grs.at[n], grs_s.at[n], grs_r.at[n], along_z(d)))

    for copy in g_rs:
        copy.wait()
    total = gsum[pl.ds(pl.multiple_of(slot * GCHUNK, GCHUNK), GCHUNK), :]
    for n in range(len(NEAR)):
        total = total + grs[n]
    gmine[...] = total
    pl.semaphore_wait(far1, 2)
    g_x = [remote(gmine, gx.at[n], gx_s.at[n], gx_r.at[n], along_z(d)) for n, d in enumerate(FAR)]

    own.wait()
    for copy in a2a:
        copy.wait()
    def put(p, cols, value):
        hi, lo = split(value)
        xs[p, pl.ds(0, COLS), cols] = hi
        xs[p, pl.ds(COLS, COLS), cols] = lo

    @pl.when(row == 2 * NZ - 1)
    def _():
        plain = cur[tail, :]
        xh, xl = split(plain)
        moved = plain - three(mm, ph[...], pl_[...], xh, xl)
        cur[tail, :] = jnp.where(c == 0, moved, plain)
        put(1, pl.ds(0, TAIL), cur[pl.ds(0, TAIL), :].T)
        put(1, tail, jnp.where(c <= 1, moved, plain).T)

    put(0, pl.ds(0, ROWS), cur[...].T)

    def inner(p):
        value = xs.at[p * end]
        both = mm(value[...], vh[p])
        w2[p] = both[:COLS] + both[COLS:] + mm(value[pl.ds(0, COLS), :], vl[p])

    halves = (0, 1)

    def half(h):
        return pl.ds(h * HALF, HALF)

    def spot(h, s):
        return pl.ds(pl.multiple_of(h * HALF + s * CHUNK, CHUNK), CHUNK)

    inner(core)
    w_p = [remote(w2.at[core, half(h), :], wpair.at[half(h), :], wp_s.at[h], wp_r.at[h], partner) for h in halves]
    inner(part)
    w_rs = []
    for h in halves:
        w_p[h].wait()
        wsum[half(h), :] = w2[part, half(h), :] + wpair[half(h), :]
        w_rs.append([
            remote(wsum.at[spot(h, slot_of(d)), :], wrs.at[h, n], wrs_s.at[h, n], wrs_r.at[h, n], along_z(d))
            for n, d in near(h)
        ])

    def prepare_t(i, _):
        rows = pl.ds(pl.multiple_of(i * R, R), R)
        for s, panel in ((0, pa), (1, pb)):
            hi, lo = split(t3[panel, rows, :])
            th[s, rows, :] = hi
            tl[s, rows, :] = lo
        return 0

    lax.fori_loop(0, PANEL // R, prepare_t, 0)
    w_x = []

    def exchange(h):
        for copy in w_rs[h]:
            copy.wait()
        total = wsum[spot(h, slot), :]
        for n in range(len(NEAR)):
            total = total + wrs[h, n]
        wmine[h] = total
        w_x.append([
            remote(wmine.at[h], wx.at[h, n], wx_s.at[h, n], wx_r.at[h, n], along_z(d))
            for n, d in enumerate(FAR)
        ])

    exchange(0)
    for copy in g_x:
        copy.wait()
    ghalf = gi * 128 + core * 64
    gspot = (pl.ds(pl.multiple_of(ghalf + final * GCHUNK, GCHUNK), GCHUNK), bj)
    gfull[gspot] = (gx[0] + gx[1]) + (gx[2] + gx[3])
    g_ag = [
        remote(gfull.at[gspot], gfull.at[gspot], gag_s.at[n], gag_r.at[n], along_z(d)) for n, d in near(1)
    ]
    exchange(1)
    for copy in g_ag:
        copy.wait()
    gown = gfull.at[pl.ds(pl.multiple_of(ghalf, 64), 64), bj]
    g_xy = [remote(gown, gown, gxy_s.at[n], gxy_r.at[n], in_plane(a, b)) for n, (a, b) in enumerate(XY)]

    w_ag = []
    for h in halves:
        for copy in w_x[h]:
            copy.wait()
        at = wfull.at[part, spot(h, final), :]
        wfull[part, spot(h, final), :] = (wx[h, 0] + wx[h, 1]) + (wx[h, 2] + wx[h, 3])
        w_ag.append([
            remote(at, at, wag_s.at[h, n], wag_r.at[h, n], along_z(d)) for n, d in near(h)
        ])
    w_c = []

    def hand_over(h):
        for copy in w_ag[h]:
            copy.wait()
        at = wfull.at[part, half(h), :]
        w_c.append(remote(at, at, wc_s.at[h], wc_r.at[h], partner))

    hand_over(0)
    for copy in g_xy:
        copy.wait()
    g_c = []
    for i in range(4):
        strip = gfull.at[pl.ds(pl.multiple_of(i * 128 + core * 64, 64), 64), :]
        g_c.append(remote(strip, strip, gc_s.at[i], gc_r.at[i], partner))
    hand_over(1)
    def update(p, value, sh, sl):
        both = mm_nt(vh[p], jnp.concatenate([sh, sl], axis=0))
        return value - (both[:, :COLS] + both[:, COLS:] + mm_nt(vl[p], sh))

    def apply_a():
        hi, lo = split(wfull[0])
        hi, lo = split(three(mm_nt, hi, lo, th[0], tl[0]))
        sah[...] = hi
        sal[...] = lo
        cur[...] = update(0, cur[...], hi, lo)

    @pl.when(core == 1)
    def _():
        apply_a()

    for copy in w_c:
        copy.wait()

    @pl.when(core == 0)
    def _():
        apply_a()

    for copy in g_c:
        copy.wait()
    gh, gl = split(gfull[...])
    hi, lo = split(wfull[1] - three(mm_nt, sah[...], sal[...], gh, gl))
    hi, lo = split(three(mm_nt, hi, lo, th[1], tl[1]))
    out_ref[...] = update(1, cur[...], hi, lo)

    @pl.when(row == 2 * NZ - 1)
    def _():
        after_b = out_ref[tail, :]
        xh, xl = split(jnp.where(c == 1, cur[tail, :], after_b))
        moved = three(mm, ph[...], pl_[...], xh, xl)
        out_ref[tail, :] = jnp.where(c == 0, after_b, after_b - moved)


def per_device(eigvecs, reflectors, t_factor, offsets):
    dma = pltpu.SemaphoreType.DMA
    near, far, plane = len(NEAR), len(FAR), len(XY)
    hbm, vmem = pl.BlockSpec(memory_space=pl.ANY), pltpu.VMEM
    return pl.pallas_call(
        kernel,
        out_shape=jax.ShapeDtypeStruct((ROWS, COLS), F32),
        in_specs=[pl.BlockSpec(memory_space=pltpu.SMEM), hbm, hbm, hbm],
        out_specs=pl.BlockSpec(memory_space=pltpu.VMEM),
        scratch_shapes=[
            vmem((PIECE, COLS * NX * NY), F32),
            vmem((ROWS, COLS), F32),
            vmem((3, ROWS, PANEL), F32),
            vmem((3, PANEL, PANEL), F32),
            vmem((3, ROWS, PANEL), BF16),
            vmem((3, ROWS, PANEL), BF16),
            vmem((PANEL, PANEL), BF16),
            vmem((PANEL, PANEL), BF16),
            vmem((3, PANEL, PANEL), BF16),
            vmem((3, PANEL, PANEL), BF16),
            vmem((PANEL, PANEL), BF16),
            vmem((PANEL, PANEL), BF16),
            vmem((2, 2 * COLS, ROWS), BF16),
            vmem((COLS, PANEL), BF16),
            vmem((COLS, PANEL), BF16),
            vmem((2, COLS, PANEL), F32),
            vmem((COLS, PANEL), F32),
            vmem((COLS, PANEL), F32),
            vmem((2, near, CHUNK, PANEL), F32),
            vmem((2, far, CHUNK, PANEL), F32),
            vmem((2, CHUNK, PANEL), F32),
            vmem((2, COLS, PANEL), F32),
            vmem((128, 128), F32),
            vmem((64, 128), F32),
            vmem((64, 128), F32),
            vmem((near, GCHUNK, 128), F32),
            vmem((far, GCHUNK, 128), F32),
            vmem((GCHUNK, 128), F32),
            vmem((PANEL, PANEL), F32),
            dma((5,)), dma, dma((plane,)), dma((plane,)), dma, dma, dma((2,)), dma((2,)),
            dma((near,)), dma((near,)), dma((2, near)), dma((2, near)),
            dma((far,)), dma((far,)), dma((2, far)), dma((2, far)),
            dma((near,)), dma((near,)), dma((2, near)), dma((2, near)),
            dma((plane,)), dma((plane,)), dma((4,)), dma((4,)), dma((2,)), dma((2,)),
            pltpu.SemaphoreType.REGULAR, pltpu.SemaphoreType.REGULAR,
        ],
        compiler_params=pltpu.CompilerParams(
            collective_id=0, has_side_effects=True, vmem_limit_bytes=54600 * 2**10
        ),
        cost_estimate=pl.CostEstimate(flops=3 * 10**9, bytes_accessed=9 * 10**6, transcendentals=0),
        name="panels",
    )(offsets, eigvecs, reflectors, t_factor)


def solution(mesh):
    return jax.shard_map(
        per_device,
        mesh=mesh,
        in_specs=(P(("row", "col"), None), P(None, "row", None), P(), P()),
        out_specs=P("row", "col"),
        check_vma=False,
    )
```

```python
import jax
import jax.numpy as jnp
from jax import lax
from jax.experimental import pallas as pl
from jax.experimental.pallas import tpu as pltpu
from jax.sharding import PartitionSpec as P

MESH = pl.DeviceIdType.MESH
F32 = jnp.float32
BF16 = jnp.bfloat16

NX, NY, NZ = 4, 4, 32
ROWS, PANEL, COLS = 768, 512, 128
PIECE = 48
TAIL = ROWS - PANEL
LAST = 64 * ROWS - PANEL
NEAR = (4, 3, -3, 2, -2, 1, -1)
FAR = (12, -12, 4, -4)
XY = tuple((a, b) for a in range(NX) for b in range(NY) if (a, b) != (0, 0))
HALF, LANES = COLS // 2, 512
PARTS = 2 * PANEL // LANES
CHUNK = HALF // 8
GCHUNK = 8


def split(value):
    hi = value.astype(BF16)
    return hi, (value - hi.astype(F32)).astype(BF16)


def mm(a, b):
    return lax.dot_general(a, b, (((1,), (0,)), ((), ())), preferred_element_type=F32)


def mm_nt(a, b):
    return lax.dot_general(a, b, (((1,), (1,)), ((), ())), preferred_element_type=F32)


def mm_tn(a, b):
    return lax.dot_general(a, b, (((0,), (0,)), ((), ())), preferred_element_type=F32)


def three(dot, ah, al, bh, bl):
    return dot(ah, bh) + (dot(ah, bl) + dot(al, bh))


def kernel(
    off_ref, x_hbm, v_hbm, t_hbm, out_ref,
    xv, cur, v3, t3, vh, vl, ch, cl, th, tl, ph, pl_, xs, sah, sal, w2, wpair, wsum, wrs, wx, wmine, wfull,
    gpart, gpair, gsum, grs, gx, gmine, gfull,
    load_sem, own_sem, a2a_s, a2a_r, gp_s, gp_r, wp_s, wp_r, grs_s, grs_r, wrs_s, wrs_r,
    gx_s, gx_r, wx_s, wx_r, gag_s, gag_r, wag_s, wag_r, gxy_s, gxy_r, gc_s, gc_r, wc_s, wc_r, far0, far1,
):
    row, col = lax.axis_index("row"), lax.axis_index("col")
    z, core = row // 2, lax.rem(row, 2)
    x, y = col // NY, lax.rem(col, NY)
    other = 1 - core
    part = 1 - core

    def along_z(d):
        return (lax.rem(z + (d + NZ), NZ) * 2 + core, col)

    def in_plane(a, b):
        return (row, lax.rem(x + a, NX) * NY + lax.rem(y + b, NY))

    partner = (z * 2 + other, col)

    def remote(src, dst, ssem, rsem, to):
        copy = pltpu.make_async_remote_copy(
            src_ref=src, dst_ref=dst, send_sem=ssem, recv_sem=rsem, device_id=to, device_id_type=MESH
        )
        copy.start()
        return copy

    barrier = pltpu.get_barrier_semaphore()
    greet = [in_plane(a, b) for a, b in XY] + [along_z(d) for d in (4, -4, 3, -3, 2, -2, 1, -1)] + [partner]
    for to in greet:
        pl.semaphore_signal(barrier, inc=1, device_id=to, device_id_type=MESH)

    xload = pltpu.make_async_copy(x_hbm, xv, load_sem.at[0])
    xload.start()
    vloads = [pltpu.make_async_copy(v_hbm.at[p], v3.at[p], load_sem.at[1 + p]) for p in range(3)]
    tload = pltpu.make_async_copy(t_hbm, t3, load_sem.at[4])
    for load in vloads:
        load.start()

    c = jnp.where(off_ref[0] == LAST, 0, jnp.where(off_ref[1] == LAST, 1, 2))
    pa = jnp.where(c == 0, 1, 0)
    pb = jnp.where(c == 2, 1, 2)
    off_a, off_b = off_ref[pa], off_ref[pb]

    def masked(panel, start, first, count):
        rows = pl.ds(first, count)
        if panel is pa:
            value = jnp.where(pa == 1, v3[1, rows, :], v3[0, rows, :])
        elif panel is pb:
            value = jnp.where(pb == 1, v3[1, rows, :], v3[2, rows, :])
        else:
            value = v3[panel, rows, :]
        step = (
            row * ROWS + first - start
            + lax.broadcasted_iota(jnp.int32, (count, PANEL), 0)
            - lax.broadcasted_iota(jnp.int32, (count, PANEL), 1)
        )
        return jnp.where(step > 0, value, jnp.where(step == 0, F32(1.0), F32(0.0)))

    mine = pl.ds(pl.multiple_of(col * PIECE, PIECE), PIECE)
    xload.wait()
    own = pltpu.make_async_copy(
        xv.at[:, pl.ds(pl.multiple_of(col * COLS, COLS), COLS)], cur.at[mine, :], own_sem
    )
    own.start()
    R = 64

    def prepare(s, panel, start):
        def some(i, _):
            first = pl.multiple_of(i * R, R)
            hi, lo = split(masked(panel, start, first, R))
            vh[s, pl.ds(first, R), :] = hi
            vl[s, pl.ds(first, R), :] = lo
            return 0

        lax.fori_loop(0, ROWS // R, some, 0)

    vloads[0].wait()
    vloads[1].wait()
    prepare(0, pa, off_a)
    pl.semaphore_wait(barrier, len(greet))
    a2a = []
    for n, (a, b) in enumerate(XY):
        to = in_plane(a, b)
        src = xv.at[:, pl.ds(pl.multiple_of(to[1] * COLS, COLS), COLS)]
        a2a.append(remote(src, cur.at[mine, :], a2a_s.at[n], a2a_r.at[n], to))
    for d in (4, -4):
        pl.semaphore_signal(far0, inc=1, device_id=along_z(d), device_id_type=MESH)

    vloads[2].wait()
    tload.start()
    prepare(1, pb, off_b)
    tail = pl.ds(TAIL, PANEL)
    end = jnp.where(row == 2 * NZ - 1, 1, 0)
    M = 128

    tload.wait()

    @pl.when(row == 2 * NZ - 1)
    def _():
        def prepare_c(i, _):
            first = pl.multiple_of(i * R, R)
            rows = pl.ds(first, R)
            hi, lo = split(masked(c, LAST, TAIL + first, R))
            ch[rows, :] = hi
            cl[rows, :] = lo
            hi, lo = split(t3[c, rows, :])
            th[2, rows, :] = hi
            tl[2, rows, :] = lo
            return 0

        lax.fori_loop(0, PANEL // R, prepare_c, 0)

        def project(i, _):
            rows = pl.ds(pl.multiple_of(i * M, M), M)
            hi, lo = split(three(mm, ch[rows, :], cl[rows, :], th[2], tl[2]))
            hi, lo = split(three(mm_nt, hi, lo, ch[...], cl[...]))
            ph[rows, :] = hi
            pl_[rows, :] = lo
            return 0

        lax.fori_loop(0, PANEL // M, project, 0)
        vh[2, pl.ds(0, TAIL), :] = vh[0, pl.ds(0, TAIL), :]
        vl[2, pl.ds(0, TAIL), :] = vl[0, pl.ds(0, TAIL), :]

        def through(i, _):
            rows = pl.ds(pl.multiple_of(i * M, M), M)
            there = pl.ds(pl.multiple_of(TAIL + i * M, M), M)
            moved = three(mm, ph[rows, :], pl_[rows, :], vh[0, tail, :], vl[0, tail, :])
            value = masked(pa, off_a, TAIL + i * M, M)
            hi, lo = split(jnp.where(c == 1, value - moved, value))
            vh[2, there, :] = hi
            vl[2, there, :] = lo
            return 0

        lax.fori_loop(0, PANEL // M, through, 0)

    gi, gj = x, y
    bi = pl.ds(pl.multiple_of(gi * 128, 128), 128)
    bj = pl.ds(pl.multiple_of(gj * 128, 128), 128)
    gpart[...] = three(mm_tn, vh[1, :, bi], vl[1, :, bi], vh[2 * end, :, bj], vl[2 * end, :, bj])
    gp = remote(gpart.at[pl.ds(pl.multiple_of(other * 64, 64), 64), :], gpair, gp_s, gp_r, partner)

    gp.wait()
    gsum[...] = gpart[pl.ds(pl.multiple_of(core * 64, 64), 64), :] + gpair[...]
    slot = lax.rem(z, 8)
    final = lax.rem(z + 4, 8)

    def near(h):
        sign = 1 - 2 * lax.rem(core + h, 2)
        return [(n, d * sign) for n, d in enumerate(NEAR)]

    def slot_of(d):
        return lax.rem(z + (d + NZ), 8)

    g_rs = []
    for n, d in near(0):
        src = gsum.at[pl.ds(pl.multiple_of(slot_of(d) * GCHUNK, GCHUNK), GCHUNK), :]
        g_rs.append(remote(src, grs.at[n], grs_s.at[n], grs_r.at[n], along_z(d)))

    pl.semaphore_wait(far0, 2)
    for d in (4, -4):
        pl.semaphore_signal(far1, inc=1, device_id=along_z(d), device_id_type=MESH)

    own.wait()
    for copy in a2a:
        copy.wait()
    def put(p, cols, value):
        hi, lo = split(value)
        xs[p, pl.ds(0, COLS), cols] = hi
        xs[p, pl.ds(COLS, COLS), cols] = lo

    @pl.when(row == 2 * NZ - 1)
    def _():
        plain = cur[tail, :]
        xh, xl = split(plain)
        moved = plain - three(mm, ph[...], pl_[...], xh, xl)
        cur[tail, :] = jnp.where(c == 0, moved, plain)
        put(1, pl.ds(0, TAIL), cur[pl.ds(0, TAIL), :].T)
        put(1, tail, jnp.where(c <= 1, moved, plain).T)

    put(0, pl.ds(0, ROWS), cur[...].T)

    def inner(p):
        value = xs.at[p * end]
        both = mm(value[...], vh[p])
        w2[p] = both[:COLS] + both[COLS:] + mm(value[pl.ds(0, COLS), :], vl[p])

    halves = tuple(range(PARTS))

    def lanes(h):
        return pl.ds(h // 2 * LANES, LANES)

    def half(h):
        return pl.ds(h % 2 * HALF, HALF), lanes(h)

    def spot(h, s):
        return pl.ds(pl.multiple_of(h % 2 * HALF + s * CHUNK, CHUNK), CHUNK), lanes(h)

    inner(core)
    w_p = [remote(w2.at[(core, *half(h))], wpair.at[half(h)], wp_s.at[h], wp_r.at[h], partner) for h in halves]
    inner(part)
    for copy in g_rs:
        copy.wait()
    total = gsum[pl.ds(pl.multiple_of(slot * GCHUNK, GCHUNK), GCHUNK), :]
    for n in range(len(NEAR)):
        total = total + grs[n]
    gmine[...] = total
    pl.semaphore_wait(far1, 2)
    g_x = [remote(gmine, gx.at[n], gx_s.at[n], gx_r.at[n], along_z(d)) for n, d in enumerate(FAR)]

    w_rs = []
    for h in halves:
        w_p[h].wait()
        wsum[half(h)] = w2[(part, *half(h))] + wpair[half(h)]
        w_rs.append([
            remote(wsum.at[spot(h, slot_of(d))], wrs.at[h, n], wrs_s.at[h, n], wrs_r.at[h, n], along_z(d))
            for n, d in near(h)
        ])

    def prepare_t(i, _):
        rows = pl.ds(pl.multiple_of(i * R, R), R)
        for s, panel in ((0, pa), (1, pb)):
            hi, lo = split(t3[panel, rows, :])
            th[s, rows, :] = hi
            tl[s, rows, :] = lo
        return 0

    lax.fori_loop(0, PANEL // R, prepare_t, 0)
    w_x = []

    def exchange(h):
        for copy in w_rs[h]:
            copy.wait()
        total = wsum[spot(h, slot)]
        for n in range(len(NEAR)):
            total = total + wrs[h, n]
        wmine[h] = total
        w_x.append([
            remote(wmine.at[h], wx.at[h, n], wx_s.at[h, n], wx_r.at[h, n], along_z(d))
            for n, d in enumerate(FAR)
        ])

    for h in halves[: PARTS // 2]:
        exchange(h)
    for copy in g_x:
        copy.wait()
    ghalf = gi * 128 + core * 64
    gspot = (pl.ds(pl.multiple_of(ghalf + final * GCHUNK, GCHUNK), GCHUNK), bj)
    gfull[gspot] = (gx[0] + gx[1]) + (gx[2] + gx[3])
    g_ag = [
        remote(gfull.at[gspot], gfull.at[gspot], gag_s.at[n], gag_r.at[n], along_z(d)) for n, d in near(1)
    ]
    for h in halves[PARTS // 2 :]:
        exchange(h)
    for copy in g_ag:
        copy.wait()
    gown = gfull.at[pl.ds(pl.multiple_of(ghalf, 64), 64), bj]
    g_xy = [remote(gown, gown, gxy_s.at[n], gxy_r.at[n], in_plane(a, b)) for n, (a, b) in enumerate(XY)]

    w_ag = []
    for h in halves:
        for copy in w_x[h]:
            copy.wait()
        at = wfull.at[(part, *spot(h, final))]
        wfull[(part, *spot(h, final))] = (wx[h, 0] + wx[h, 1]) + (wx[h, 2] + wx[h, 3])
        w_ag.append([
            remote(at, at, wag_s.at[h, n], wag_r.at[h, n], along_z(d)) for n, d in near(h)
        ])
    w_c = []

    def hand_over(h):
        for copy in w_ag[h]:
            copy.wait()
        at = wfull.at[(part, *half(h))]
        w_c.append(remote(at, at, wc_s.at[h], wc_r.at[h], partner))

    for h in halves[:-1]:
        hand_over(h)
    for copy in g_xy:
        copy.wait()
    g_c = []
    for i in range(4):
        strip = gfull.at[pl.ds(pl.multiple_of(i * 128 + core * 64, 64), 64), :]
        g_c.append(remote(strip, strip, gc_s.at[i], gc_r.at[i], partner))
    hand_over(halves[-1])
    def update(p, value, sh, sl):
        both = mm_nt(vh[p], jnp.concatenate([sh, sl], axis=0))
        return value - (both[:, :COLS] + both[:, COLS:] + mm_nt(vl[p], sh))

    def apply_a():
        hi, lo = split(wfull[0])
        hi, lo = split(three(mm_nt, hi, lo, th[0], tl[0]))
        sah[...] = hi
        sal[...] = lo
        cur[...] = update(0, cur[...], hi, lo)

    @pl.when(core == 1)
    def _():
        apply_a()

    for copy in w_c:
        copy.wait()

    @pl.when(core == 0)
    def _():
        apply_a()

    for copy in g_c:
        copy.wait()
    gh, gl = split(gfull[...])
    hi, lo = split(wfull[1] - three(mm_nt, sah[...], sal[...], gh, gl))
    hi, lo = split(three(mm_nt, hi, lo, th[1], tl[1]))
    out_ref[...] = update(1, cur[...], hi, lo)

    @pl.when(row == 2 * NZ - 1)
    def _():
        after_b = out_ref[tail, :]
        xh, xl = split(jnp.where(c == 1, cur[tail, :], after_b))
        moved = three(mm, ph[...], pl_[...], xh, xl)
        out_ref[tail, :] = jnp.where(c == 0, after_b, after_b - moved)


def per_device(eigvecs, reflectors, t_factor, offsets):
    dma = pltpu.SemaphoreType.DMA
    near, far, plane = len(NEAR), len(FAR), len(XY)
    hbm, vmem = pl.BlockSpec(memory_space=pl.ANY), pltpu.VMEM
    return pl.pallas_call(
        kernel,
        out_shape=jax.ShapeDtypeStruct((ROWS, COLS), F32),
        in_specs=[pl.BlockSpec(memory_space=pltpu.SMEM), hbm, hbm, hbm],
        out_specs=pl.BlockSpec(memory_space=pltpu.VMEM),
        scratch_shapes=[
            vmem((PIECE, COLS * NX * NY), F32),
            vmem((ROWS, COLS), F32),
            vmem((3, ROWS, PANEL), F32),
            vmem((3, PANEL, PANEL), F32),
            vmem((3, ROWS, PANEL), BF16),
            vmem((3, ROWS, PANEL), BF16),
            vmem((PANEL, PANEL), BF16),
            vmem((PANEL, PANEL), BF16),
            vmem((3, PANEL, PANEL), BF16),
            vmem((3, PANEL, PANEL), BF16),
            vmem((PANEL, PANEL), BF16),
            vmem((PANEL, PANEL), BF16),
            vmem((2, 2 * COLS, ROWS), BF16),
            vmem((COLS, PANEL), BF16),
            vmem((COLS, PANEL), BF16),
            vmem((2, COLS, PANEL), F32),
            vmem((COLS, PANEL), F32),
            vmem((COLS, PANEL), F32),
            vmem((PARTS, near, CHUNK, LANES), F32),
            vmem((PARTS, far, CHUNK, LANES), F32),
            vmem((PARTS, CHUNK, LANES), F32),
            vmem((2, COLS, PANEL), F32),
            vmem((128, 128), F32),
            vmem((64, 128), F32),
            vmem((64, 128), F32),
            vmem((near, GCHUNK, 128), F32),
            vmem((far, GCHUNK, 128), F32),
            vmem((GCHUNK, 128), F32),
            vmem((PANEL, PANEL), F32),
            dma((5,)), dma, dma((plane,)), dma((plane,)), dma, dma, dma((PARTS,)), dma((PARTS,)),
            dma((near,)), dma((near,)), dma((PARTS, near)), dma((PARTS, near)),
            dma((far,)), dma((far,)), dma((PARTS, far)), dma((PARTS, far)),
            dma((near,)), dma((near,)), dma((PARTS, near)), dma((PARTS, near)),
            dma((plane,)), dma((plane,)), dma((4,)), dma((4,)), dma((PARTS,)), dma((PARTS,)),
            pltpu.SemaphoreType.REGULAR, pltpu.SemaphoreType.REGULAR,
        ],
        compiler_params=pltpu.CompilerParams(
            collective_id=0, has_side_effects=True, vmem_limit_bytes=54600 * 2**10
        ),
        cost_estimate=pl.CostEstimate(flops=3 * 10**9, bytes_accessed=9 * 10**6, transcendentals=0),
        name="panels",
    )(offsets, eigvecs, reflectors, t_factor)


def solution(mesh):
    return jax.shard_map(
        per_device,
        mesh=mesh,
        in_specs=(P(("row", "col"), None), P(None, "row", None), P(), P()),
        out_specs=P("row", "col"),
        check_vma=False,
    )
```

```python
import jax
import jax.numpy as jnp
from jax import lax
from jax.experimental import pallas as pl
from jax.experimental.pallas import tpu as pltpu
from jax.sharding import PartitionSpec as P

MESH = pl.DeviceIdType.MESH
F32 = jnp.float32
BF16 = jnp.bfloat16

NX, NY, NZ = 4, 4, 32
ROWS, PANEL, COLS = 768, 512, 128
PIECE = 48
TAIL = ROWS - PANEL
LAST = 64 * ROWS - PANEL
NEAR = (4, 3, -3, 2, -2, 1, -1)
FAR = (12, -12, 4, -4)
XY = tuple((a, b) for a in range(NX) for b in range(NY) if (a, b) != (0, 0))
HALF, LANES = COLS // 2, 256
PARTS = 2 * PANEL // LANES
CHUNK = HALF // 8
GCHUNK = 8


def split(value):
    hi = value.astype(BF16)
    return hi, (value - hi.astype(F32)).astype(BF16)


def mm(a, b):
    return lax.dot_general(a, b, (((1,), (0,)), ((), ())), preferred_element_type=F32)


def mm_nt(a, b):
    return lax.dot_general(a, b, (((1,), (1,)), ((), ())), preferred_element_type=F32)


def mm_tn(a, b):
    return lax.dot_general(a, b, (((0,), (0,)), ((), ())), preferred_element_type=F32)


def three(dot, ah, al, bh, bl):
    return dot(ah, bh) + (dot(ah, bl) + dot(al, bh))


def kernel(
    off_ref, x_hbm, v_hbm, t_hbm, out_ref,
    xv, cur, v3, t3, vh, vl, ch, cl, th, tl, ph, pl_, xs, gh, gl, sag, w2, wpair, wsum, wrs, wx, wmine, wfull,
    gpart, gpair, gsum, grs, gx, gmine, gfull,
    load_sem, own_sem, a2a_s, a2a_r, gp_s, gp_r, wp_s, wp_r, grs_s, grs_r, wrs_s, wrs_r,
    gx_s, gx_r, wx_s, wx_r, gag_s, gag_r, wag_s, wag_r, gxy_s, gxy_r, gc_s, gc_r, wc_s, wc_r, far0, far1,
):
    row, col = lax.axis_index("row"), lax.axis_index("col")
    z, core = row // 2, lax.rem(row, 2)
    x, y = col // NY, lax.rem(col, NY)
    other = 1 - core
    part = 1 - core

    def along_z(d):
        return (lax.rem(z + (d + NZ), NZ) * 2 + core, col)

    def in_plane(a, b):
        return (row, lax.rem(x + a, NX) * NY + lax.rem(y + b, NY))

    partner = (z * 2 + other, col)

    def remote(src, dst, ssem, rsem, to):
        copy = pltpu.make_async_remote_copy(
            src_ref=src, dst_ref=dst, send_sem=ssem, recv_sem=rsem, device_id=to, device_id_type=MESH
        )
        copy.start()
        return copy

    barrier = pltpu.get_barrier_semaphore()
    greet = [in_plane(a, b) for a, b in XY] + [along_z(d) for d in (4, -4, 3, -3, 2, -2, 1, -1)] + [partner]
    for to in greet:
        pl.semaphore_signal(barrier, inc=1, device_id=to, device_id_type=MESH)

    xload = pltpu.make_async_copy(x_hbm, xv, load_sem.at[0])
    xload.start()
    vloads = [pltpu.make_async_copy(v_hbm.at[p], v3.at[p], load_sem.at[1 + p]) for p in range(3)]
    tload = pltpu.make_async_copy(t_hbm, t3, load_sem.at[4])
    for load in vloads:
        load.start()

    c = jnp.where(off_ref[0] == LAST, 0, jnp.where(off_ref[1] == LAST, 1, 2))
    pa = jnp.where(c == 0, 1, 0)
    pb = jnp.where(c == 2, 1, 2)
    off_a, off_b = off_ref[pa], off_ref[pb]

    def masked(panel, start, first, count):
        rows = pl.ds(first, count)
        if panel is pa:
            value = jnp.where(pa == 1, v3[1, rows, :], v3[0, rows, :])
        elif panel is pb:
            value = jnp.where(pb == 1, v3[1, rows, :], v3[2, rows, :])
        else:
            value = v3[panel, rows, :]
        step = (
            row * ROWS + first - start
            + lax.broadcasted_iota(jnp.int32, (count, PANEL), 0)
            - lax.broadcasted_iota(jnp.int32, (count, PANEL), 1)
        )
        return jnp.where(step > 0, value, jnp.where(step == 0, F32(1.0), F32(0.0)))

    mine = pl.ds(pl.multiple_of(col * PIECE, PIECE), PIECE)
    xload.wait()
    own = pltpu.make_async_copy(
        xv.at[:, pl.ds(pl.multiple_of(col * COLS, COLS), COLS)], cur.at[mine, :], own_sem
    )
    own.start()
    R = 64

    def prepare(s, panel, start):
        def some(i, _):
            first = pl.multiple_of(i * R, R)
            hi, lo = split(masked(panel, start, first, R))
            vh[s, pl.ds(first, R), :] = hi
            vl[s, pl.ds(first, R), :] = lo
            return 0

        lax.fori_loop(0, ROWS // R, some, 0)

    vloads[0].wait()
    vloads[1].wait()
    prepare(0, pa, off_a)
    pl.semaphore_wait(barrier, len(greet))
    a2a = []
    for n, (a, b) in enumerate(XY):
        to = in_plane(a, b)
        src = xv.at[:, pl.ds(pl.multiple_of(to[1] * COLS, COLS), COLS)]
        a2a.append(remote(src, cur.at[mine, :], a2a_s.at[n], a2a_r.at[n], to))
    for d in (4, -4):
        pl.semaphore_signal(far0, inc=1, device_id=along_z(d), device_id_type=MESH)

    vloads[2].wait()
    tload.start()
    prepare(1, pb, off_b)
    tail = pl.ds(TAIL, PANEL)
    end = jnp.where(row == 2 * NZ - 1, 1, 0)
    M = 128

    tload.wait()

    @pl.when(row == 2 * NZ - 1)
    def _():
        def prepare_c(i, _):
            first = pl.multiple_of(i * R, R)
            rows = pl.ds(first, R)
            hi, lo = split(masked(c, LAST, TAIL + first, R))
            ch[rows, :] = hi
            cl[rows, :] = lo
            hi, lo = split(t3[c, rows, :])
            th[2, rows, :] = hi
            tl[2, rows, :] = lo
            return 0

        lax.fori_loop(0, PANEL // R, prepare_c, 0)

        def project(i, _):
            rows = pl.ds(pl.multiple_of(i * M, M), M)
            hi, lo = split(three(mm, ch[rows, :], cl[rows, :], th[2], tl[2]))
            hi, lo = split(three(mm_nt, hi, lo, ch[...], cl[...]))
            ph[rows, :] = hi
            pl_[rows, :] = lo
            return 0

        lax.fori_loop(0, PANEL // M, project, 0)
        vh[2, pl.ds(0, TAIL), :] = vh[0, pl.ds(0, TAIL), :]
        vl[2, pl.ds(0, TAIL), :] = vl[0, pl.ds(0, TAIL), :]

        def through(i, _):
            rows = pl.ds(pl.multiple_of(i * M, M), M)
            there = pl.ds(pl.multiple_of(TAIL + i * M, M), M)
            moved = three(mm, ph[rows, :], pl_[rows, :], vh[0, tail, :], vl[0, tail, :])
            value = masked(pa, off_a, TAIL + i * M, M)
            hi, lo = split(jnp.where(c == 1, value - moved, value))
            vh[2, there, :] = hi
            vl[2, there, :] = lo
            return 0

        lax.fori_loop(0, PANEL // M, through, 0)

    gi, gj = x, y
    bi = pl.ds(pl.multiple_of(gi * 128, 128), 128)
    bj = pl.ds(pl.multiple_of(gj * 128, 128), 128)
    gpart[...] = three(mm_tn, vh[1, :, bi], vl[1, :, bi], vh[2 * end, :, bj], vl[2 * end, :, bj])
    gp = remote(gpart.at[pl.ds(pl.multiple_of(other * 64, 64), 64), :], gpair, gp_s, gp_r, partner)

    gp.wait()
    gsum[...] = gpart[pl.ds(pl.multiple_of(core * 64, 64), 64), :] + gpair[...]
    slot = lax.rem(z, 8)
    final = lax.rem(z + 4, 8)

    def near(h):
        sign = 1 - 2 * lax.rem(core + h, 2)
        return [(n, d * sign) for n, d in enumerate(NEAR)]

    def slot_of(d):
        return lax.rem(z + (d + NZ), 8)

    g_rs = []
    for n, d in near(0):
        src = gsum.at[pl.ds(pl.multiple_of(slot_of(d) * GCHUNK, GCHUNK), GCHUNK), :]
        g_rs.append(remote(src, grs.at[n], grs_s.at[n], grs_r.at[n], along_z(d)))

    pl.semaphore_wait(far0, 2)
    for d in (4, -4):
        pl.semaphore_signal(far1, inc=1, device_id=along_z(d), device_id_type=MESH)

    own.wait()
    for copy in a2a:
        copy.wait()
    def put(p, cols, value):
        hi, lo = split(value)
        xs[p, pl.ds(0, COLS), cols] = hi
        xs[p, pl.ds(COLS, COLS), cols] = lo

    @pl.when(row == 2 * NZ - 1)
    def _():
        plain = cur[tail, :]
        xh, xl = split(plain)
        moved = plain - three(mm, ph[...], pl_[...], xh, xl)
        cur[tail, :] = jnp.where(c == 0, moved, plain)
        put(1, pl.ds(0, TAIL), cur[pl.ds(0, TAIL), :].T)
        put(1, tail, jnp.where(c <= 1, moved, plain).T)

    put(0, pl.ds(0, ROWS), cur[...].T)

    def inner(p):
        value = xs.at[p * end]
        both = mm(value[...], vh[p])
        w2[p] = both[:COLS] + both[COLS:] + mm(value[pl.ds(0, COLS), :], vl[p])

    halves = tuple(range(PARTS))

    def lanes(h):
        return pl.ds(h // 2 * LANES, LANES)

    def half(h):
        return pl.ds(h % 2 * HALF, HALF), lanes(h)

    def spot(h, s):
        return pl.ds(pl.multiple_of(h % 2 * HALF + s * CHUNK, CHUNK), CHUNK), lanes(h)

    inner(core)
    w_p = [remote(w2.at[(core, *half(h))], wpair.at[half(h)], wp_s.at[h], wp_r.at[h], partner) for h in halves]
    inner(part)
    for copy in g_rs:
        copy.wait()
    total = gsum[pl.ds(pl.multiple_of(slot * GCHUNK, GCHUNK), GCHUNK), :]
    for n in range(len(NEAR)):
        total = total + grs[n]
    gmine[...] = total
    pl.semaphore_wait(far1, 2)
    g_x = [remote(gmine, gx.at[n], gx_s.at[n], gx_r.at[n], along_z(d)) for n, d in enumerate(FAR)]

    w_rs = []
    for h in halves:
        w_p[h].wait()
        wsum[half(h)] = w2[(part, *half(h))] + wpair[half(h)]
        w_rs.append([
            remote(wsum.at[spot(h, slot_of(d))], wrs.at[h, n], wrs_s.at[h, n], wrs_r.at[h, n], along_z(d))
            for n, d in near(h)
        ])

    def prepare_t(i, _):
        rows = pl.ds(pl.multiple_of(i * R, R), R)
        for s, panel in ((0, pa), (1, pb)):
            hi, lo = split(t3[panel, rows, :])
            th[s, rows, :] = hi
            tl[s, rows, :] = lo
        return 0

    lax.fori_loop(0, PANEL // R, prepare_t, 0)
    w_x = []

    def exchange(h):
        for copy in w_rs[h]:
            copy.wait()
        total = wsum[spot(h, slot)]
        for n in range(len(NEAR)):
            total = total + wrs[h, n]
        wmine[h] = total
        w_x.append([
            remote(wmine.at[h], wx.at[h, n], wx_s.at[h, n], wx_r.at[h, n], along_z(d))
            for n, d in enumerate(FAR)
        ])

    for h in halves[: PARTS // 2]:
        exchange(h)
    for copy in g_x:
        copy.wait()
    ghalf = gi * 128 + core * 64
    gspot = (pl.ds(pl.multiple_of(ghalf + final * GCHUNK, GCHUNK), GCHUNK), bj)
    gfull[gspot] = (gx[0] + gx[1]) + (gx[2] + gx[3])
    g_ag = [
        remote(gfull.at[gspot], gfull.at[gspot], gag_s.at[n], gag_r.at[n], along_z(d)) for n, d in near(1)
    ]
    for h in halves[PARTS // 2 :]:
        exchange(h)
    for copy in g_ag:
        copy.wait()
    gown = gfull.at[pl.ds(pl.multiple_of(ghalf, 64), 64), bj]
    g_xy = [remote(gown, gown, gxy_s.at[n], gxy_r.at[n], in_plane(a, b)) for n, (a, b) in enumerate(XY)]

    w_ag = []
    for h in halves:
        for copy in w_x[h]:
            copy.wait()
        at = wfull.at[(part, *spot(h, final))]
        wfull[(part, *spot(h, final))] = (wx[h, 0] + wx[h, 1]) + (wx[h, 2] + wx[h, 3])
        w_ag.append([
            remote(at, at, wag_s.at[h, n], wag_r.at[h, n], along_z(d)) for n, d in near(h)
        ])
    w_c = []

    def hand_over(h):
        for copy in w_ag[h]:
            copy.wait()
        at = wfull.at[(part, *half(h))]
        w_c.append(remote(at, at, wc_s.at[h], wc_r.at[h], partner))

    for h in halves[:-1]:
        hand_over(h)
    for copy in g_xy:
        copy.wait()
    g_c = []
    for i in range(4):
        strip = gfull.at[pl.ds(pl.multiple_of(i * 128 + core * 64, 64), 64), :]
        g_c.append(remote(strip, strip, gc_s.at[i], gc_r.at[i], partner))
    hand_over(halves[-1])
    def update(p, value, sh, sl):
        both = mm_nt(vh[p], jnp.concatenate([sh, sl], axis=0))
        return value - (both[:, :COLS] + both[:, COLS:] + mm_nt(vl[p], sh))

    def apply_a():
        hi, lo = split(wfull[0])
        hi, lo = split(three(mm_nt, hi, lo, th[0], tl[0]))
        sag[...] = three(mm_nt, hi, lo, gh[...], gl[...])
        cur[...] = update(0, cur[...], hi, lo)

    for copy in g_c:
        copy.wait()
    gh[...], gl[...] = split(gfull[...])

    @pl.when(core == 1)
    def _():
        apply_a()

    for copy in w_c:
        copy.wait()

    @pl.when(core == 0)
    def _():
        apply_a()

    hi, lo = split(wfull[1] - sag[...])
    hi, lo = split(three(mm_nt, hi, lo, th[1], tl[1]))
    out_ref[...] = update(1, cur[...], hi, lo)

    @pl.when(row == 2 * NZ - 1)
    def _():
        after_b = out_ref[tail, :]
        xh, xl = split(jnp.where(c == 1, cur[tail, :], after_b))
        moved = three(mm, ph[...], pl_[...], xh, xl)
        out_ref[tail, :] = jnp.where(c == 0, after_b, after_b - moved)


def per_device(eigvecs, reflectors, t_factor, offsets):
    dma = pltpu.SemaphoreType.DMA
    near, far, plane = len(NEAR), len(FAR), len(XY)
    hbm, vmem = pl.BlockSpec(memory_space=pl.ANY), pltpu.VMEM
    return pl.pallas_call(
        kernel,
        out_shape=jax.ShapeDtypeStruct((ROWS, COLS), F32),
        in_specs=[pl.BlockSpec(memory_space=pltpu.SMEM), hbm, hbm, hbm],
        out_specs=pl.BlockSpec(memory_space=pltpu.VMEM),
        scratch_shapes=[
            vmem((PIECE, COLS * NX * NY), F32),
            vmem((ROWS, COLS), F32),
            vmem((3, ROWS, PANEL), F32),
            vmem((3, PANEL, PANEL), F32),
            vmem((3, ROWS, PANEL), BF16),
            vmem((3, ROWS, PANEL), BF16),
            vmem((PANEL, PANEL), BF16),
            vmem((PANEL, PANEL), BF16),
            vmem((3, PANEL, PANEL), BF16),
            vmem((3, PANEL, PANEL), BF16),
            vmem((PANEL, PANEL), BF16),
            vmem((PANEL, PANEL), BF16),
            vmem((2, 2 * COLS, ROWS), BF16),
            vmem((PANEL, PANEL), BF16),
            vmem((PANEL, PANEL), BF16),
            vmem((COLS, PANEL), F32),
            vmem((2, COLS, PANEL), F32),
            vmem((COLS, PANEL), F32),
            vmem((COLS, PANEL), F32),
            vmem((PARTS, near, CHUNK, LANES), F32),
            vmem((PARTS, far, CHUNK, LANES), F32),
            vmem((PARTS, CHUNK, LANES), F32),
            vmem((2, COLS, PANEL), F32),
            vmem((128, 128), F32),
            vmem((64, 128), F32),
            vmem((64, 128), F32),
            vmem((near, GCHUNK, 128), F32),
            vmem((far, GCHUNK, 128), F32),
            vmem((GCHUNK, 128), F32),
            vmem((PANEL, PANEL), F32),
            dma((5,)), dma, dma((plane,)), dma((plane,)), dma, dma, dma((PARTS,)), dma((PARTS,)),
            dma((near,)), dma((near,)), dma((PARTS, near)), dma((PARTS, near)),
            dma((far,)), dma((far,)), dma((PARTS, far)), dma((PARTS, far)),
            dma((near,)), dma((near,)), dma((PARTS, near)), dma((PARTS, near)),
            dma((plane,)), dma((plane,)), dma((4,)), dma((4,)), dma((PARTS,)), dma((PARTS,)),
            pltpu.SemaphoreType.REGULAR, pltpu.SemaphoreType.REGULAR,
        ],
        compiler_params=pltpu.CompilerParams(
            collective_id=0, has_side_effects=True, vmem_limit_bytes=54600 * 2**10
        ),
        cost_estimate=pl.CostEstimate(flops=3 * 10**9, bytes_accessed=9 * 10**6, transcendentals=0),
        name="panels",
    )(offsets, eigvecs, reflectors, t_factor)


def solution(mesh):
    return jax.shard_map(
        per_device,
        mesh=mesh,
        in_specs=(P(("row", "col"), None), P(None, "row", None), P(), P()),
        out_specs=P("row", "col"),
        check_vma=False,
    )
```

```python
import jax
import jax.numpy as jnp
from jax import lax
from jax.experimental import pallas as pl
from jax.experimental.pallas import tpu as pltpu
from jax.sharding import PartitionSpec as P

MESH = pl.DeviceIdType.MESH
F32 = jnp.float32
BF16 = jnp.bfloat16

NX, NY, NZ = 4, 4, 32
ROWS, PANEL, COLS = 768, 512, 128
PIECE = 48
TAIL = ROWS - PANEL
LAST = 64 * ROWS - PANEL
NEAR = (4, 3, -3, 2, -2, 1, -1)
FAR = (12, -12, 4, -4)
XY = tuple((a, b) for a in range(NX) for b in range(NY) if (a, b) != (0, 0))
HALF, LANES = COLS // 2, 512
PARTS = 2 * PANEL // LANES
CHUNK = HALF // 8
GCHUNK = 8


def split(value):
    hi = value.astype(BF16)
    return hi, (value - hi.astype(F32)).astype(BF16)


def mm(a, b):
    return lax.dot_general(a, b, (((1,), (0,)), ((), ())), preferred_element_type=F32)


def mm_nt(a, b):
    return lax.dot_general(a, b, (((1,), (1,)), ((), ())), preferred_element_type=F32)


def mm_tn(a, b):
    return lax.dot_general(a, b, (((0,), (0,)), ((), ())), preferred_element_type=F32)


def three(dot, ah, al, bh, bl):
    return dot(ah, bh) + (dot(ah, bl) + dot(al, bh))


def kernel(
    off_ref, x_hbm, v_hbm, t_hbm, out_ref,
    xv, cur, v3, t3, vh, vl, ch, cl, th, tl, ph, pl_, xs, gh, gl, sag, w2, wpair, wsum, wrs, wx, wmine, wfull,
    gpart, gpair, gsum, grs, gx, gmine, gfull,
    load_sem, own_sem, a2a_s, a2a_r, gp_s, gp_r, wp_s, wp_r, grs_s, grs_r, wrs_s, wrs_r,
    gx_s, gx_r, wx_s, wx_r, gag_s, gag_r, wag_s, wag_r, gxy_s, gxy_r, gc_s, gc_r, wc_s, wc_r, far0, far1,
):
    row, col = lax.axis_index("row"), lax.axis_index("col")
    z, core = row // 2, lax.rem(row, 2)
    x, y = col // NY, lax.rem(col, NY)
    other = 1 - core
    part = 1 - core

    def along_z(d):
        return (lax.rem(z + (d + NZ), NZ) * 2 + core, col)

    def in_plane(a, b):
        return (row, lax.rem(x + a, NX) * NY + lax.rem(y + b, NY))

    partner = (z * 2 + other, col)

    sent = []

    def remote(src, dst, ssem, rsem, to):
        copy = pltpu.make_async_remote_copy(
            src_ref=src, dst_ref=dst, send_sem=ssem, recv_sem=rsem, device_id=to, device_id_type=MESH
        )
        copy.start()
        sent.append(copy)
        return copy

    barrier = pltpu.get_barrier_semaphore()
    greet = [in_plane(a, b) for a, b in XY] + [along_z(d) for d in (4, -4, 3, -3, 2, -2, 1, -1)] + [partner]
    for to in greet:
        pl.semaphore_signal(barrier, inc=1, device_id=to, device_id_type=MESH)

    xload = pltpu.make_async_copy(x_hbm, xv, load_sem.at[0])
    xload.start()
    vloads = [pltpu.make_async_copy(v_hbm.at[p], v3.at[p], load_sem.at[1 + p]) for p in range(3)]
    tload = pltpu.make_async_copy(t_hbm, t3, load_sem.at[4])
    for load in vloads:
        load.start()

    c = jnp.where(off_ref[0] == LAST, 0, jnp.where(off_ref[1] == LAST, 1, 2))
    pa = jnp.where(c == 0, 1, 0)
    pb = jnp.where(c == 2, 1, 2)
    off_a, off_b = off_ref[pa], off_ref[pb]

    def masked(panel, start, first, count):
        rows = pl.ds(first, count)
        if panel is pa:
            value = jnp.where(pa == 1, v3[1, rows, :], v3[0, rows, :])
        elif panel is pb:
            value = jnp.where(pb == 1, v3[1, rows, :], v3[2, rows, :])
        else:
            value = v3[panel, rows, :]
        step = (
            row * ROWS + first - start
            + lax.broadcasted_iota(jnp.int32, (count, PANEL), 0)
            - lax.broadcasted_iota(jnp.int32, (count, PANEL), 1)
        )
        return jnp.where(step > 0, value, jnp.where(step == 0, F32(1.0), F32(0.0)))

    mine = pl.ds(pl.multiple_of(col * PIECE, PIECE), PIECE)
    xload.wait()
    own = pltpu.make_async_copy(
        xv.at[:, pl.ds(pl.multiple_of(col * COLS, COLS), COLS)], cur.at[mine, :], own_sem
    )
    own.start()
    R = 64

    def prepare(s, panel, start):
        def some(i, _):
            first = pl.multiple_of(i * R, R)
            hi, lo = split(masked(panel, start, first, R))
            vh[s, pl.ds(first, R), :] = hi
            vl[s, pl.ds(first, R), :] = lo
            return 0

        lax.fori_loop(0, ROWS // R, some, 0)

    vloads[0].wait()
    vloads[1].wait()
    prepare(0, pa, off_a)
    pl.semaphore_wait(barrier, len(greet))
    a2a = []
    for n, (a, b) in enumerate(XY):
        to = in_plane(a, b)
        src = xv.at[:, pl.ds(pl.multiple_of(to[1] * COLS, COLS), COLS)]
        a2a.append(remote(src, cur.at[mine, :], a2a_s.at[n], a2a_r.at[n], to))
    for d in (4, -4):
        pl.semaphore_signal(far0, inc=1, device_id=along_z(d), device_id_type=MESH)

    vloads[2].wait()
    tload.start()
    prepare(1, pb, off_b)
    tail = pl.ds(TAIL, PANEL)
    end = jnp.where(row == 2 * NZ - 1, 1, 0)
    M = 128

    tload.wait()

    @pl.when(row == 2 * NZ - 1)
    def _():
        def prepare_c(i, _):
            first = pl.multiple_of(i * R, R)
            rows = pl.ds(first, R)
            hi, lo = split(masked(c, LAST, TAIL + first, R))
            ch[rows, :] = hi
            cl[rows, :] = lo
            hi, lo = split(t3[c, rows, :])
            th[2, rows, :] = hi
            tl[2, rows, :] = lo
            return 0

        lax.fori_loop(0, PANEL // R, prepare_c, 0)

        def project(i, _):
            rows = pl.ds(pl.multiple_of(i * M, M), M)
            hi, lo = split(three(mm, ch[rows, :], cl[rows, :], th[2], tl[2]))
            hi, lo = split(three(mm_nt, hi, lo, ch[...], cl[...]))
            ph[rows, :] = hi
            pl_[rows, :] = lo
            return 0

        lax.fori_loop(0, PANEL // M, project, 0)
        vh[2, pl.ds(0, TAIL), :] = vh[0, pl.ds(0, TAIL), :]
        vl[2, pl.ds(0, TAIL), :] = vl[0, pl.ds(0, TAIL), :]

        def through(i, _):
            rows = pl.ds(pl.multiple_of(i * M, M), M)
            there = pl.ds(pl.multiple_of(TAIL + i * M, M), M)
            moved = three(mm, ph[rows, :], pl_[rows, :], vh[0, tail, :], vl[0, tail, :])
            value = masked(pa, off_a, TAIL + i * M, M)
            hi, lo = split(jnp.where(c == 1, value - moved, value))
            vh[2, there, :] = hi
            vl[2, there, :] = lo
            return 0

        lax.fori_loop(0, PANEL // M, through, 0)

    gi, gj = x, y
    bi = pl.ds(pl.multiple_of(gi * 128, 128), 128)
    bj = pl.ds(pl.multiple_of(gj * 128, 128), 128)
    gpart[...] = three(mm_tn, vh[1, :, bi], vl[1, :, bi], vh[2 * end, :, bj], vl[2 * end, :, bj])
    gp = remote(gpart.at[pl.ds(pl.multiple_of(other * 64, 64), 64), :], gpair, gp_s, gp_r, partner)

    gp.wait_recv()
    gsum[...] = gpart[pl.ds(pl.multiple_of(core * 64, 64), 64), :] + gpair[...]
    slot = lax.rem(z, 8)
    final = lax.rem(z + 4, 8)

    def near(h):
        sign = 1 - 2 * lax.rem(core + h, 2)
        return [(n, d * sign) for n, d in enumerate(NEAR)]

    def slot_of(d):
        return lax.rem(z + (d + NZ), 8)

    g_rs = []
    for n, d in near(0):
        src = gsum.at[pl.ds(pl.multiple_of(slot_of(d) * GCHUNK, GCHUNK), GCHUNK), :]
        g_rs.append(remote(src, grs.at[n], grs_s.at[n], grs_r.at[n], along_z(d)))

    pl.semaphore_wait(far0, 2)
    for d in (4, -4):
        pl.semaphore_signal(far1, inc=1, device_id=along_z(d), device_id_type=MESH)

    own.wait()
    for copy in a2a:
        copy.wait_recv()
    def put(p, cols, value):
        hi, lo = split(value)
        xs[p, pl.ds(0, COLS), cols] = hi
        xs[p, pl.ds(COLS, COLS), cols] = lo

    @pl.when(row == 2 * NZ - 1)
    def _():
        plain = cur[tail, :]
        xh, xl = split(plain)
        moved = plain - three(mm, ph[...], pl_[...], xh, xl)
        cur[tail, :] = jnp.where(c == 0, moved, plain)
        put(1, pl.ds(0, TAIL), cur[pl.ds(0, TAIL), :].T)
        put(1, tail, jnp.where(c <= 1, moved, plain).T)

    put(0, pl.ds(0, ROWS), cur[...].T)

    def inner(p):
        value = xs.at[p * end]
        both = mm(value[...], vh[p])
        w2[p] = both[:COLS] + both[COLS:] + mm(value[pl.ds(0, COLS), :], vl[p])

    halves = tuple(range(PARTS))

    def lanes(h):
        return pl.ds(h // 2 * LANES, LANES)

    def half(h):
        return pl.ds(h % 2 * HALF, HALF), lanes(h)

    def spot(h, s):
        return pl.ds(pl.multiple_of(h % 2 * HALF + s * CHUNK, CHUNK), CHUNK), lanes(h)

    inner(core)
    w_p = [remote(w2.at[(core, *half(h))], wpair.at[half(h)], wp_s.at[h], wp_r.at[h], partner) for h in halves]
    inner(part)
    for copy in g_rs:
        copy.wait_recv()
    total = gsum[pl.ds(pl.multiple_of(slot * GCHUNK, GCHUNK), GCHUNK), :]
    for n in range(len(NEAR)):
        total = total + grs[n]
    gmine[...] = total
    pl.semaphore_wait(far1, 2)
    g_x = [remote(gmine, gx.at[n], gx_s.at[n], gx_r.at[n], along_z(d)) for n, d in enumerate(FAR)]

    w_rs = []
    for h in halves:
        w_p[h].wait_recv()
        wsum[half(h)] = w2[(part, *half(h))] + wpair[half(h)]
        w_rs.append([
            remote(wsum.at[spot(h, slot_of(d))], wrs.at[h, n], wrs_s.at[h, n], wrs_r.at[h, n], along_z(d))
            for n, d in near(h)
        ])

    def prepare_t(i, _):
        rows = pl.ds(pl.multiple_of(i * R, R), R)
        for s, panel in ((0, pa), (1, pb)):
            hi, lo = split(t3[panel, rows, :])
            th[s, rows, :] = hi
            tl[s, rows, :] = lo
        return 0

    lax.fori_loop(0, PANEL // R, prepare_t, 0)
    w_x = []

    def exchange(h):
        for copy in w_rs[h]:
            copy.wait_recv()
        total = wsum[spot(h, slot)]
        for n in range(len(NEAR)):
            total = total + wrs[h, n]
        wmine[h] = total
        w_x.append([
            remote(wmine.at[h], wx.at[h, n], wx_s.at[h, n], wx_r.at[h, n], along_z(d))
            for n, d in enumerate(FAR)
        ])

    for h in halves[: PARTS // 2]:
        exchange(h)
    for copy in g_x:
        copy.wait_recv()
    ghalf = gi * 128 + core * 64
    gspot = (pl.ds(pl.multiple_of(ghalf + final * GCHUNK, GCHUNK), GCHUNK), bj)
    gfull[gspot] = (gx[0] + gx[1]) + (gx[2] + gx[3])
    g_ag = [
        remote(gfull.at[gspot], gfull.at[gspot], gag_s.at[n], gag_r.at[n], along_z(d)) for n, d in near(1)
    ]
    for h in halves[PARTS // 2 :]:
        exchange(h)
    for copy in g_ag:
        copy.wait_recv()
    gown = gfull.at[pl.ds(pl.multiple_of(ghalf, 64), 64), bj]
    g_xy = [remote(gown, gown, gxy_s.at[n], gxy_r.at[n], in_plane(a, b)) for n, (a, b) in enumerate(XY)]

    w_ag = []
    for h in halves:
        for copy in w_x[h]:
            copy.wait_recv()
        at = wfull.at[(part, *spot(h, final))]
        wfull[(part, *spot(h, final))] = (wx[h, 0] + wx[h, 1]) + (wx[h, 2] + wx[h, 3])
        w_ag.append([
            remote(at, at, wag_s.at[h, n], wag_r.at[h, n], along_z(d)) for n, d in near(h)
        ])
    w_c = []

    def hand_over(h):
        for copy in w_ag[h]:
            copy.wait_recv()
        at = wfull.at[(part, *half(h))]
        w_c.append(remote(at, at, wc_s.at[h], wc_r.at[h], partner))

    for h in halves[:-1]:
        hand_over(h)
    for copy in g_xy:
        copy.wait_recv()
    g_c = []
    for i in range(4):
        strip = gfull.at[pl.ds(pl.multiple_of(i * 128 + core * 64, 64), 64), :]
        g_c.append(remote(strip, strip, gc_s.at[i], gc_r.at[i], partner))
    hand_over(halves[-1])
    def update(p, value, sh, sl):
        both = mm_nt(vh[p], jnp.concatenate([sh, sl], axis=0))
        return value - (both[:, :COLS] + both[:, COLS:] + mm_nt(vl[p], sh))

    def apply_a():
        hi, lo = split(wfull[0])
        hi, lo = split(three(mm_nt, hi, lo, th[0], tl[0]))
        sag[...] = three(mm_nt, hi, lo, gh[...], gl[...])
        cur[...] = update(0, cur[...], hi, lo)

    for copy in g_c:
        copy.wait_recv()
    gh[...], gl[...] = split(gfull[...])

    @pl.when(core == 1)
    def _():
        apply_a()

    for copy in w_c:
        copy.wait_recv()

    @pl.when(core == 0)
    def _():
        apply_a()

    hi, lo = split(wfull[1] - sag[...])
    hi, lo = split(three(mm_nt, hi, lo, th[1], tl[1]))
    out_ref[...] = update(1, cur[...], hi, lo)

    @pl.when(row == 2 * NZ - 1)
    def _():
        after_b = out_ref[tail, :]
        xh, xl = split(jnp.where(c == 1, cur[tail, :], after_b))
        moved = three(mm, ph[...], pl_[...], xh, xl)
        out_ref[tail, :] = jnp.where(c == 0, after_b, after_b - moved)

    for copy in sent:
        copy.wait_send()


def per_device(eigvecs, reflectors, t_factor, offsets):
    dma = pltpu.SemaphoreType.DMA
    near, far, plane = len(NEAR), len(FAR), len(XY)
    hbm, vmem = pl.BlockSpec(memory_space=pl.ANY), pltpu.VMEM
    return pl.pallas_call(
        kernel,
        out_shape=jax.ShapeDtypeStruct((ROWS, COLS), F32),
        in_specs=[pl.BlockSpec(memory_space=pltpu.SMEM), hbm, hbm, hbm],
        out_specs=pl.BlockSpec(memory_space=pltpu.VMEM),
        scratch_shapes=[
            vmem((PIECE, COLS * NX * NY), F32),
            vmem((ROWS, COLS), F32),
            vmem((3, ROWS, PANEL), F32),
            vmem((3, PANEL, PANEL), F32),
            vmem((3, ROWS, PANEL), BF16),
            vmem((3, ROWS, PANEL), BF16),
            vmem((PANEL, PANEL), BF16),
            vmem((PANEL, PANEL), BF16),
            vmem((3, PANEL, PANEL), BF16),
            vmem((3, PANEL, PANEL), BF16),
            vmem((PANEL, PANEL), BF16),
            vmem((PANEL, PANEL), BF16),
            vmem((2, 2 * COLS, ROWS), BF16),
            vmem((PANEL, PANEL), BF16),
            vmem((PANEL, PANEL), BF16),
            vmem((COLS, PANEL), F32),
            vmem((2, COLS, PANEL), F32),
            vmem((COLS, PANEL), F32),
            vmem((COLS, PANEL), F32),
            vmem((PARTS, near, CHUNK, LANES), F32),
            vmem((PARTS, far, CHUNK, LANES), F32),
            vmem((PARTS, CHUNK, LANES), F32),
            vmem((2, COLS, PANEL), F32),
            vmem((128, 128), F32),
            vmem((64, 128), F32),
            vmem((64, 128), F32),
            vmem((near, GCHUNK, 128), F32),
            vmem((far, GCHUNK, 128), F32),
            vmem((GCHUNK, 128), F32),
            vmem((PANEL, PANEL), F32),
            dma((5,)), dma, dma((plane,)), dma((plane,)), dma, dma, dma((PARTS,)), dma((PARTS,)),
            dma((near,)), dma((near,)), dma((PARTS, near)), dma((PARTS, near)),
            dma((far,)), dma((far,)), dma((PARTS, far)), dma((PARTS, far)),
            dma((near,)), dma((near,)), dma((PARTS, near)), dma((PARTS, near)),
            dma((plane,)), dma((plane,)), dma((4,)), dma((4,)), dma((PARTS,)), dma((PARTS,)),
            pltpu.SemaphoreType.REGULAR, pltpu.SemaphoreType.REGULAR,
        ],
        compiler_params=pltpu.CompilerParams(
            collective_id=0, has_side_effects=True, vmem_limit_bytes=54600 * 2**10
        ),
        cost_estimate=pl.CostEstimate(flops=3 * 10**9, bytes_accessed=9 * 10**6, transcendentals=0),
        name="panels",
    )(offsets, eigvecs, reflectors, t_factor)


def solution(mesh):
    return jax.shard_map(
        per_device,
        mesh=mesh,
        in_specs=(P(("row", "col"), None), P(None, "row", None), P(), P()),
        out_specs=P("row", "col"),
        check_vma=False,
    )
```

```python
import jax
import jax.numpy as jnp
from jax import lax
from jax.experimental import pallas as pl
from jax.experimental.pallas import tpu as pltpu
from jax.sharding import PartitionSpec as P

MESH = pl.DeviceIdType.MESH
F32 = jnp.float32
BF16 = jnp.bfloat16

NX, NY, NZ = 4, 4, 32
ROWS, PANEL, COLS = 768, 512, 128
PIECE = 48
TAIL = ROWS - PANEL
LAST = 64 * ROWS - PANEL
NEAR = (4, 3, -3, 2, -2, 1, -1)
FAR = (12, -12, 4, -4)
XY = sorted(
    ((a, b) for a in range(NX) for b in range(NY) if (a, b) != (0, 0)),
    key=lambda p: (-min(p[0], NX - p[0]) - min(p[1], NY - p[1]), p),
)
HALF, LANES = COLS // 2, 512
PARTS = 2 * PANEL // LANES
CHUNK = HALF // 8
GCHUNK = 8


def split(value):
    hi = value.astype(BF16)
    return hi, (value - hi.astype(F32)).astype(BF16)


def mm(a, b):
    return lax.dot_general(a, b, (((1,), (0,)), ((), ())), preferred_element_type=F32)


def mm_nt(a, b):
    return lax.dot_general(a, b, (((1,), (1,)), ((), ())), preferred_element_type=F32)


def mm_tn(a, b):
    return lax.dot_general(a, b, (((0,), (0,)), ((), ())), preferred_element_type=F32)


def three(dot, ah, al, bh, bl):
    return dot(ah, bh) + (dot(ah, bl) + dot(al, bh))


def kernel(
    off_ref, x_hbm, v_hbm, t_hbm, out_ref,
    xv, cur, v3, t3, vh, vl, ch, cl, th, tl, ph, pl_, xs, gh, gl, sag, w2, wpair, wsum, wrs, wx, wmine, wfull,
    gpart, gpair, gsum, grs, gx, gmine, gfull,
    load_sem, own_sem, a2a_s, a2a_r, gp_s, gp_r, wp_s, wp_r, grs_s, grs_r, wrs_s, wrs_r,
    gx_s, gx_r, wx_s, wx_r, gag_s, gag_r, wag_s, wag_r, gxy_s, gxy_r, gc_s, gc_r, wc_s, wc_r, far0, far1,
):
    row, col = lax.axis_index("row"), lax.axis_index("col")
    z, core = row // 2, lax.rem(row, 2)
    x, y = col // NY, lax.rem(col, NY)
    other = 1 - core
    part = 1 - core

    def along_z(d):
        return (lax.rem(z + (d + NZ), NZ) * 2 + core, col)

    def in_plane(a, b):
        return (row, lax.rem(x + a, NX) * NY + lax.rem(y + b, NY))

    partner = (z * 2 + other, col)

    sent = []

    def remote(src, dst, ssem, rsem, to):
        copy = pltpu.make_async_remote_copy(
            src_ref=src, dst_ref=dst, send_sem=ssem, recv_sem=rsem, device_id=to, device_id_type=MESH
        )
        copy.start()
        sent.append(copy)
        return copy

    barrier = pltpu.get_barrier_semaphore()
    greet = [in_plane(a, b) for a, b in XY] + [along_z(d) for d in (4, -4, 3, -3, 2, -2, 1, -1)] + [partner]
    for to in greet:
        pl.semaphore_signal(barrier, inc=1, device_id=to, device_id_type=MESH)

    xload = pltpu.make_async_copy(x_hbm, xv, load_sem.at[0])
    xload.start()
    vloads = [pltpu.make_async_copy(v_hbm.at[p], v3.at[p], load_sem.at[1 + p]) for p in range(3)]
    tload = pltpu.make_async_copy(t_hbm, t3, load_sem.at[4])
    for load in vloads:
        load.start()

    c = jnp.where(off_ref[0] == LAST, 0, jnp.where(off_ref[1] == LAST, 1, 2))
    pa = jnp.where(c == 0, 1, 0)
    pb = jnp.where(c == 2, 1, 2)
    off_a, off_b = off_ref[pa], off_ref[pb]

    def masked(panel, start, first, count):
        rows = pl.ds(first, count)
        if panel is pa:
            value = jnp.where(pa == 1, v3[1, rows, :], v3[0, rows, :])
        elif panel is pb:
            value = jnp.where(pb == 1, v3[1, rows, :], v3[2, rows, :])
        else:
            value = v3[panel, rows, :]
        step = (
            row * ROWS + first - start
            + lax.broadcasted_iota(jnp.int32, (count, PANEL), 0)
            - lax.broadcasted_iota(jnp.int32, (count, PANEL), 1)
        )
        return jnp.where(step > 0, value, jnp.where(step == 0, F32(1.0), F32(0.0)))

    mine = pl.ds(pl.multiple_of(col * PIECE, PIECE), PIECE)
    xload.wait()
    own = pltpu.make_async_copy(
        xv.at[:, pl.ds(pl.multiple_of(col * COLS, COLS), COLS)], cur.at[mine, :], own_sem
    )
    own.start()
    R = 64

    def prepare(s, panel, start):
        def some(i, _):
            first = pl.multiple_of(i * R, R)
            hi, lo = split(masked(panel, start, first, R))
            vh[s, pl.ds(first, R), :] = hi
            vl[s, pl.ds(first, R), :] = lo
            return 0

        lax.fori_loop(0, ROWS // R, some, 0)

    vloads[0].wait()
    vloads[1].wait()
    prepare(0, pa, off_a)
    pl.semaphore_wait(barrier, len(greet))
    a2a = []
    for n, (a, b) in enumerate(XY):
        to = in_plane(a, b)
        src = xv.at[:, pl.ds(pl.multiple_of(to[1] * COLS, COLS), COLS)]
        a2a.append(remote(src, cur.at[mine, :], a2a_s.at[n], a2a_r.at[n], to))
    for d in (4, -4):
        pl.semaphore_signal(far0, inc=1, device_id=along_z(d), device_id_type=MESH)

    vloads[2].wait()
    tload.start()
    prepare(1, pb, off_b)
    tail = pl.ds(TAIL, PANEL)
    end = jnp.where(row == 2 * NZ - 1, 1, 0)
    M = 128

    tload.wait()

    @pl.when(row == 2 * NZ - 1)
    def _():
        def prepare_c(i, _):
            first = pl.multiple_of(i * R, R)
            rows = pl.ds(first, R)
            hi, lo = split(masked(c, LAST, TAIL + first, R))
            ch[rows, :] = hi
            cl[rows, :] = lo
            hi, lo = split(t3[c, rows, :])
            th[2, rows, :] = hi
            tl[2, rows, :] = lo
            return 0

        lax.fori_loop(0, PANEL // R, prepare_c, 0)

        def project(i, _):
            rows = pl.ds(pl.multiple_of(i * M, M), M)
            hi, lo = split(three(mm, ch[rows, :], cl[rows, :], th[2], tl[2]))
            hi, lo = split(three(mm_nt, hi, lo, ch[...], cl[...]))
            ph[rows, :] = hi
            pl_[rows, :] = lo
            return 0

        lax.fori_loop(0, PANEL // M, project, 0)
        vh[2, pl.ds(0, TAIL), :] = vh[0, pl.ds(0, TAIL), :]
        vl[2, pl.ds(0, TAIL), :] = vl[0, pl.ds(0, TAIL), :]

        def through(i, _):
            rows = pl.ds(pl.multiple_of(i * M, M), M)
            there = pl.ds(pl.multiple_of(TAIL + i * M, M), M)
            moved = three(mm, ph[rows, :], pl_[rows, :], vh[0, tail, :], vl[0, tail, :])
            value = masked(pa, off_a, TAIL + i * M, M)
            hi, lo = split(jnp.where(c == 1, value - moved, value))
            vh[2, there, :] = hi
            vl[2, there, :] = lo
            return 0

        lax.fori_loop(0, PANEL // M, through, 0)

    gi, gj = x, y
    bi = pl.ds(pl.multiple_of(gi * 128, 128), 128)
    bj = pl.ds(pl.multiple_of(gj * 128, 128), 128)
    gpart[...] = three(mm_tn, vh[1, :, bi], vl[1, :, bi], vh[2 * end, :, bj], vl[2 * end, :, bj])
    gp = remote(gpart.at[pl.ds(pl.multiple_of(other * 64, 64), 64), :], gpair, gp_s, gp_r, partner)

    gp.wait_recv()
    gsum[...] = gpart[pl.ds(pl.multiple_of(core * 64, 64), 64), :] + gpair[...]
    slot = lax.rem(z, 8)
    final = lax.rem(z + 4, 8)

    def near(h):
        sign = 1 - 2 * lax.rem(core + h, 2)
        return [(n, d * sign) for n, d in enumerate(NEAR)]

    def slot_of(d):
        return lax.rem(z + (d + NZ), 8)

    g_rs = []
    for n, d in near(0):
        src = gsum.at[pl.ds(pl.multiple_of(slot_of(d) * GCHUNK, GCHUNK), GCHUNK), :]
        g_rs.append(remote(src, grs.at[n], grs_s.at[n], grs_r.at[n], along_z(d)))

    pl.semaphore_wait(far0, 2)
    for d in (4, -4):
        pl.semaphore_signal(far1, inc=1, device_id=along_z(d), device_id_type=MESH)

    own.wait()
    for copy in a2a:
        copy.wait_recv()
    def put(p, cols, value):
        hi, lo = split(value)
        xs[p, pl.ds(0, COLS), cols] = hi
        xs[p, pl.ds(COLS, COLS), cols] = lo

    @pl.when(row == 2 * NZ - 1)
    def _():
        plain = cur[tail, :]
        xh, xl = split(plain)
        moved = plain - three(mm, ph[...], pl_[...], xh, xl)
        cur[tail, :] = jnp.where(c == 0, moved, plain)
        put(1, pl.ds(0, TAIL), cur[pl.ds(0, TAIL), :].T)
        put(1, tail, jnp.where(c <= 1, moved, plain).T)

    put(0, pl.ds(0, ROWS), cur[...].T)

    def inner(p):
        value = xs.at[p * end]
        both = mm(value[...], vh[p])
        w2[p] = both[:COLS] + both[COLS:] + mm(value[pl.ds(0, COLS), :], vl[p])

    halves = tuple(range(PARTS))

    def lanes(h):
        return pl.ds(h // 2 * LANES, LANES)

    def half(h):
        return pl.ds(h % 2 * HALF, HALF), lanes(h)

    def spot(h, s):
        return pl.ds(pl.multiple_of(h % 2 * HALF + s * CHUNK, CHUNK), CHUNK), lanes(h)

    inner(core)
    w_p = [remote(w2.at[(core, *half(h))], wpair.at[half(h)], wp_s.at[h], wp_r.at[h], partner) for h in halves]
    inner(part)
    for copy in g_rs:
        copy.wait_recv()
    total = gsum[pl.ds(pl.multiple_of(slot * GCHUNK, GCHUNK), GCHUNK), :]
    for n in range(len(NEAR)):
        total = total + grs[n]
    gmine[...] = total
    pl.semaphore_wait(far1, 2)
    g_x = [remote(gmine, gx.at[n], gx_s.at[n], gx_r.at[n], along_z(d)) for n, d in enumerate(FAR)]

    w_rs = []
    for h in halves:
        w_p[h].wait_recv()
        wsum[half(h)] = w2[(part, *half(h))] + wpair[half(h)]
        w_rs.append([
            remote(wsum.at[spot(h, slot_of(d))], wrs.at[h, n], wrs_s.at[h, n], wrs_r.at[h, n], along_z(d))
            for n, d in near(h)
        ])

    def prepare_t(i, _):
        rows = pl.ds(pl.multiple_of(i * R, R), R)
        for s, panel in ((0, pa), (1, pb)):
            hi, lo = split(t3[panel, rows, :])
            th[s, rows, :] = hi
            tl[s, rows, :] = lo
        return 0

    lax.fori_loop(0, PANEL // R, prepare_t, 0)
    w_x = []

    def exchange(h):
        for copy in w_rs[h]:
            copy.wait_recv()
        total = wsum[spot(h, slot)]
        for n in range(len(NEAR)):
            total = total + wrs[h, n]
        wmine[h] = total
        w_x.append([
            remote(wmine.at[h], wx.at[h, n], wx_s.at[h, n], wx_r.at[h, n], along_z(d))
            for n, d in enumerate(FAR)
        ])

    for h in halves[: PARTS // 2]:
        exchange(h)
    for copy in g_x:
        copy.wait_recv()
    ghalf = gi * 128 + core * 64
    gspot = (pl.ds(pl.multiple_of(ghalf + final * GCHUNK, GCHUNK), GCHUNK), bj)
    gfull[gspot] = (gx[0] + gx[1]) + (gx[2] + gx[3])
    g_ag = [
        remote(gfull.at[gspot], gfull.at[gspot], gag_s.at[n], gag_r.at[n], along_z(d)) for n, d in near(1)
    ]
    for h in halves[PARTS // 2 :]:
        exchange(h)
    for copy in g_ag:
        copy.wait_recv()
    gown = gfull.at[pl.ds(pl.multiple_of(ghalf, 64), 64), bj]
    g_xy = [remote(gown, gown, gxy_s.at[n], gxy_r.at[n], in_plane(a, b)) for n, (a, b) in enumerate(XY)]

    w_ag = []
    for h in halves:
        for copy in w_x[h]:
            copy.wait_recv()
        at = wfull.at[(part, *spot(h, final))]
        wfull[(part, *spot(h, final))] = (wx[h, 0] + wx[h, 1]) + (wx[h, 2] + wx[h, 3])
        w_ag.append([
            remote(at, at, wag_s.at[h, n], wag_r.at[h, n], along_z(d)) for n, d in near(h)
        ])
    w_c = []

    def hand_over(h):
        for copy in w_ag[h]:
            copy.wait_recv()
        at = wfull.at[(part, *half(h))]
        w_c.append(remote(at, at, wc_s.at[h], wc_r.at[h], partner))

    for h in halves[:-1]:
        hand_over(h)
    for copy in g_xy:
        copy.wait_recv()
    g_c = []
    for i in range(4):
        strip = gfull.at[pl.ds(pl.multiple_of(i * 128 + core * 64, 64), 64), :]
        g_c.append(remote(strip, strip, gc_s.at[i], gc_r.at[i], partner))
    hand_over(halves[-1])
    def update(p, value, sh, sl):
        both = mm_nt(vh[p], jnp.concatenate([sh, sl], axis=0))
        return value - (both[:, :COLS] + both[:, COLS:] + mm_nt(vl[p], sh))

    def apply_a():
        hi, lo = split(wfull[0])
        hi, lo = split(three(mm_nt, hi, lo, th[0], tl[0]))
        sag[...] = three(mm_nt, hi, lo, gh[...], gl[...])
        cur[...] = update(0, cur[...], hi, lo)

    for copy in g_c:
        copy.wait_recv()
    gh[...], gl[...] = split(gfull[...])

    @pl.when(core == 1)
    def _():
        apply_a()

    for copy in w_c:
        copy.wait_recv()

    @pl.when(core == 0)
    def _():
        apply_a()

    hi, lo = split(wfull[1] - sag[...])
    hi, lo = split(three(mm_nt, hi, lo, th[1], tl[1]))
    out_ref[...] = update(1, cur[...], hi, lo)

    @pl.when(row == 2 * NZ - 1)
    def _():
        after_b = out_ref[tail, :]
        xh, xl = split(jnp.where(c == 1, cur[tail, :], after_b))
        moved = three(mm, ph[...], pl_[...], xh, xl)
        out_ref[tail, :] = jnp.where(c == 0, after_b, after_b - moved)

    for copy in sent:
        copy.wait_send()


def per_device(eigvecs, reflectors, t_factor, offsets):
    dma = pltpu.SemaphoreType.DMA
    near, far, plane = len(NEAR), len(FAR), len(XY)
    hbm, vmem = pl.BlockSpec(memory_space=pl.ANY), pltpu.VMEM
    return pl.pallas_call(
        kernel,
        out_shape=jax.ShapeDtypeStruct((ROWS, COLS), F32),
        in_specs=[pl.BlockSpec(memory_space=pltpu.SMEM), hbm, hbm, hbm],
        out_specs=pl.BlockSpec(memory_space=pltpu.VMEM),
        scratch_shapes=[
            vmem((PIECE, COLS * NX * NY), F32),
            vmem((ROWS, COLS), F32),
            vmem((3, ROWS, PANEL), F32),
            vmem((3, PANEL, PANEL), F32),
            vmem((3, ROWS, PANEL), BF16),
            vmem((3, ROWS, PANEL), BF16),
            vmem((PANEL, PANEL), BF16),
            vmem((PANEL, PANEL), BF16),
            vmem((3, PANEL, PANEL), BF16),
            vmem((3, PANEL, PANEL), BF16),
            vmem((PANEL, PANEL), BF16),
            vmem((PANEL, PANEL), BF16),
            vmem((2, 2 * COLS, ROWS), BF16),
            vmem((PANEL, PANEL), BF16),
            vmem((PANEL, PANEL), BF16),
            vmem((COLS, PANEL), F32),
            vmem((2, COLS, PANEL), F32),
            vmem((COLS, PANEL), F32),
            vmem((COLS, PANEL), F32),
            vmem((PARTS, near, CHUNK, LANES), F32),
            vmem((PARTS, far, CHUNK, LANES), F32),
            vmem((PARTS, CHUNK, LANES), F32),
            vmem((2, COLS, PANEL), F32),
            vmem((128, 128), F32),
            vmem((64, 128), F32),
            vmem((64, 128), F32),
            vmem((near, GCHUNK, 128), F32),
            vmem((far, GCHUNK, 128), F32),
            vmem((GCHUNK, 128), F32),
            vmem((PANEL, PANEL), F32),
            dma((5,)), dma, dma((plane,)), dma((plane,)), dma, dma, dma((PARTS,)), dma((PARTS,)),
            dma((near,)), dma((near,)), dma((PARTS, near)), dma((PARTS, near)),
            dma((far,)), dma((far,)), dma((PARTS, far)), dma((PARTS, far)),
            dma((near,)), dma((near,)), dma((PARTS, near)), dma((PARTS, near)),
            dma((plane,)), dma((plane,)), dma((4,)), dma((4,)), dma((PARTS,)), dma((PARTS,)),
            pltpu.SemaphoreType.REGULAR, pltpu.SemaphoreType.REGULAR,
        ],
        compiler_params=pltpu.CompilerParams(
            collective_id=0, has_side_effects=True, vmem_limit_bytes=54600 * 2**10
        ),
        cost_estimate=pl.CostEstimate(flops=3 * 10**9, bytes_accessed=9 * 10**6, transcendentals=0),
        name="panels",
    )(offsets, eigvecs, reflectors, t_factor)


def solution(mesh):
    return jax.shard_map(
        per_device,
        mesh=mesh,
        in_specs=(P(("row", "col"), None), P(None, "row", None), P(), P()),
        out_specs=P("row", "col"),
        check_vma=False,
    )
```
